32 devices in a mesh: tm: 32 (over z, y, x, core).
Axes of the slice: x: 2, y: 2, z: 4, core: 2. Of those that a mesh axis runs over, the one named last changes fastest.
Arguments:
- observations: float32 [1024, 4, 64], P('tm'), may hold values from -6 to 6
- decay: float32 [1024, 128], P('tm'), may hold values from 0 to 1
- transition: float32 [128, 128], replicated, may hold values from -1 to 1
- obs_map: float32 [64, 128], replicated, may hold values from -0.0625 to 0.0625
- noise_precision: float32 [64], replicated, may hold values from 0.01 to 0.2
- smoother_gain: float32 [128, 128], replicated, may hold values from -1 to 1
Outputs:
- filtered: float32 [1024, 4, 128], P('tm')
- smoothed: float32 [1024, 4, 128], P('tm')
The draws below stay inside these ranges and needn't reach their ends.
All inputs are finite; a program needn't handle non-finite values.
Results may differ from the reference program's by a relative error of at most 0.0003.
Values sent between devices are 32-bit elements; how exact they have to be, the bound alone decides.
A program may use at most 128 MiB of HBM per device.

```python
import math
import jax
import jax.numpy as jnp
import numpy as np
from jax import lax

S = 128
M = 64
SEQS = 4
TOTAL_EPOCHS = 1024


def butterfly(key):
    matrix = jnp.eye(S, dtype=jnp.float32)
    indices = np.arange(S)
    for level in range(S.bit_length() - 1):
        partner = indices ^ 1 << level
        lower = np.minimum(indices, partner)
        signs = np.where(indices < partner, -1.0, 1.0).astype(np.float32)
        angles = jax.random.uniform(jax.random.fold_in(key, level), (S,), jnp.float32, -math.pi, math.pi)
        paired = angles[lower]
        cosine = jnp.cos(paired)[:, None]
        sine = (jnp.sin(paired) * signs)[:, None]
        matrix = cosine * matrix + sine * matrix[partner]
    return matrix


def draw_transition(key, part):
    return butterfly(jax.random.fold_in(key, 11))


def draw_smoother_gain(key, part):
    return butterfly(jax.random.fold_in(key, 23))


def draw_decay(key, part):
    share = 1.0 / 16.0
    fast = jax.random.uniform(jax.random.fold_in(key, 31), (S,), jnp.float32) < share
    slow_rate = jnp.exp(jax.random.uniform(jax.random.fold_in(key, 32), (S,), jnp.float32, math.log(0.2 / TOTAL_EPOCHS), math.log(1.0 / TOTAL_EPOCHS)))
    fast_rate = jax.random.uniform(jax.random.fold_in(key, 33), (S,), jnp.float32, 1.0 / 50.0, 1.0 / 30.0)
    acquisition_frequency = jnp.where(fast, fast_rate, slow_rate)
    random_perturbation = jnp.exp(jax.random.uniform(jax.random.fold_in(key, 34), (TOTAL_EPOCHS, S), jnp.float32, math.log(0.5), math.log(2.0)))
    spike_present = jax.random.uniform(jax.random.fold_in(key, 35), (TOTAL_EPOCHS, 1), jnp.float32) < 6.0 / TOTAL_EPOCHS
    waveform_amplitude = jax.random.uniform(jax.random.fold_in(key, 36), (TOTAL_EPOCHS, 1), jnp.float32, 0.5, 0.8)
    spike_occurrence = jnp.where(spike_present, waveform_amplitude, 1.0)
    return jnp.exp(-acquisition_frequency[None, :] * random_perturbation) * spike_occurrence


def block_levels(own_key, shape, cuts, least, high):
    level = 1.0
    for axis_at, blocks in cuts:
        draws = jax.random.uniform(jax.random.fold_in(jax.random.fold_in(own_key, 6), axis_at), (blocks,), jnp.float32, least / len(cuts), high / len(cuts))
        level = level * jnp.repeat(jnp.exp(draws), shape[axis_at] // blocks).reshape((-1,) + (1,) * (len(shape) - 1 - axis_at))
    return level


def noise(stream_key, shape, spread, reach, pieces=(), kind=jnp.bfloat16):
    entries = jax.random.normal(stream_key, shape, jnp.float32) * spread
    if len(pieces) > 0:
        entries = block_levels(stream_key, shape, pieces, -0.22, 0.18) * entries
    return jnp.clip(entries, min=-reach, max=reach).astype(kind)


def setup_inputs(seed: int = 0) -> dict:
    arg_keys = jax.random.split(jax.random.key(seed), 7)
    observations = noise(arg_keys[0], (TOTAL_EPOCHS, SEQS, M), 1.0, 6.0, ((0, 32),), jnp.float32)
    decay = draw_decay(jax.random.fold_in(arg_keys[6], 71), 0)
    transition = draw_transition(jax.random.fold_in(arg_keys[6], 71), 0)
    obs_map = noise(arg_keys[3], (M, S), (64 * S) ** -0.5, 0.0625, (), jnp.float32)
    noise_precision = jnp.clip(jnp.exp(jax.random.uniform(arg_keys[4], (M,), jnp.float32, math.log(0.01), math.log(0.2))), 0.01, 0.2)
    smoother_gain = draw_smoother_gain(jax.random.fold_in(arg_keys[6], 71), 0)
    return dict(observations=observations, decay=decay, transition=transition, obs_map=obs_map, noise_precision=noise_precision, smoother_gain=smoother_gain)


def reference(observations, decay, transition, obs_map, noise_precision, smoother_gain):
    highest_level = lax.Precision.HIGHEST
    gain_row_block = obs_map * noise_precision[:, None]
    closed_rows = transition.T - jnp.dot(transition.T, jnp.dot(obs_map.T, gain_row_block, precision=highest_level), precision=highest_level)

    def forward(state, item):
        retain, measured = item
        state = jnp.dot(state * retain, closed_rows, precision=highest_level) + jnp.dot(measured, gain_row_block, precision=highest_level)
        return state, state

    start = jnp.zeros((SEQS, S), jnp.float32)
    _, filtered = lax.scan(forward, start, (decay, observations))
    attenuation_upcoming = jnp.concatenate([decay[1:], jnp.zeros((1, S), jnp.float32)], 0)

    def backward(state, item):
        current, retain = item
        predicted = jnp.dot(current * retain, transition.T, precision=highest_level)
        state = current + jnp.dot((state - predicted) * retain, smoother_gain.T, precision=highest_level)
        return state, state

    _, smoothed = lax.scan(backward, start, (filtered, attenuation_upcoming), reverse=True)
    return filtered, smoothed
```

```python
import functools

import jax
import jax.numpy as jnp
from jax import lax
from jax.experimental import pallas as pl
from jax.experimental.pallas import tpu as pltpu
from jax.sharding import PartitionSpec as P

MESH = pl.DeviceIdType.MESH
F32, BF16 = jnp.float32, jnp.bfloat16
S = 128
Q = 4
SUBS = 4


def halves(x):
    high = x.astype(BF16)
    low = (x - high.astype(F32)).astype(BF16)
    return jnp.concatenate([high, low], axis=1)


def weights(m):
    both = halves(m)
    return jnp.concatenate([both, both], axis=0)


def mul(x, w):
    y = jnp.dot(halves(x), w, preferred_element_type=F32)
    return y[:, :S] + y[:, S:]


def spread(row, rows):
    return jnp.broadcast_to(row, (rows, S))


def padded(x):
    return jnp.concatenate([x, jnp.zeros((8 - x.shape[0], S), F32)], axis=0)


def parts(m):
    return m[:S], m[S : S + 8], m[S + 8 :]


def compose(earlier, later):
    later_map, later_add, later_decay = parts(later)
    y = mul(earlier[: S + 8] * later_decay[:1], weights(later_map))
    return jnp.concatenate([y[:S], y[S:] + later_add, earlier[S + 8 :]], axis=0)


def pick(index, options):
    chosen = options[0]
    for k in range(1, len(options)):
        chosen = jnp.where(index == k, options[k], chosen)
    return chosen


def kernel(
    n,
    levels,
    obs_ref,
    dec_ref,
    trans_ref,
    map_ref,
    noise_ref,
    gain_ref,
    filt_ref,
    smooth_ref,
    u_ref,
    dx_ref,
    g_ref,
    next_ref,
    next_send,
    next_recv,
    *rest,
):
    count = len(levels)
    f_bufs, z_bufs, y_bufs = rest[:count], rest[count : 2 * count], rest[2 * count : 3 * count]
    send_sem, recv_sem = rest[3 * count :]
    me = lax.axis_index("tm")
    steps = dec_ref.shape[0]
    length = steps // SUBS
    digits = [(me // stride) % radix for radix, stride in levels]

    barrier = pltpu.get_barrier_semaphore()
    greeted = 0
    for (radix, stride), digit in zip(levels, digits):
        for ahead in range(1, radix):
            other = me + ((digit + ahead) % radix - digit) * stride
            pl.semaphore_signal(barrier, inc=1, device_id=(other,), device_id_type=MESH)
            greeted += 1
    pl.semaphore_signal(barrier, inc=1, device_id=((me + 1) % n,), device_id_type=MESH)
    greeted += 1

    def send(which, level, bufs, own):
        radix, stride = levels[level]
        digit = digits[level]
        bufs[level][digit] = own
        copies = []
        for ahead in range(1, radix):
            other = me + ((digit + ahead) % radix - digit) * stride
            copy = pltpu.make_async_remote_copy(
                src_ref=bufs[level].at[digit],
                dst_ref=bufs[level].at[digit],
                send_sem=send_sem.at[which, level, ahead - 1],
                recv_sem=recv_sem.at[which, level, ahead - 1],
                device_id=(other,),
                device_id_type=MESH,
            )
            copy.start()
            copies.append(copy)
        sent.extend(copies)
        return copies

    sent = []
    highest = lax.Precision.HIGHEST
    trans_t, gain_t = trans_ref[...].T, gain_ref[...].T
    obs_map, noise = map_ref[...], noise_ref[...]
    closed = trans_t - jnp.dot(
        trans_t,
        jnp.dot(obs_map.T * noise, obs_map, precision=highest, preferred_element_type=F32),
        precision=highest,
        preferred_element_type=F32,
    )
    w_closed, w_gain, w_trans = weights(closed), weights(gain_t), weights(trans_t)
    u_ref[...] = jnp.dot(
        obs_ref[...] * noise, obs_map, precision=highest, preferred_element_type=F32
    )
    dec = [dec_ref[t : t + 1, :] for t in range(steps)]
    for t in range(steps):
        dx_ref[t * Q : (t + 1) * Q, :] = spread(dec[t], Q)

    def at(ref, i):
        return jnp.concatenate(
            [ref[(b * length + i) * Q : (b * length + i + 1) * Q, :] for b in range(SUBS)], axis=0
        )

    def decayed(x, i):
        return [x[b * S : (b + 1) * S] * dec[b * length + i] for b in range(SUBS)]

    maps = jnp.concatenate([closed] * SUBS, axis=0)
    adds = at(u_ref, 0)
    back = jnp.concatenate([gain_t] * SUBS, axis=0)
    for i in range(1, length):
        y = mul(jnp.concatenate(decayed(maps, i) + [adds * at(dx_ref, i)], axis=0), w_closed)
        maps, adds = y[: SUBS * S], y[SUBS * S :] + at(u_ref, i)
        back = mul(jnp.concatenate(decayed(back, length - i), axis=0), w_gain)
    sub = [
        jnp.concatenate(
            [
                maps[b * S : (b + 1) * S],
                padded(adds[b * Q : (b + 1) * Q]),
                spread(dec[b * length], 8),
            ],
            axis=0,
        )
        for b in range(SUBS)
    ]
    sub_back = decayed(back, 0)
    total = compose(compose(sub[0], sub[1]), compose(sub[2], sub[3]))

    pl.semaphore_wait(barrier, greeted)
    waiting = send(0, 0, f_bufs, total)
    next_copy = pltpu.make_async_remote_copy(
        src_ref=dec_ref.at[pl.ds(0, 8)],
        dst_ref=next_ref,
        send_sem=next_send,
        recv_sem=next_recv,
        device_id=((me + n - 1) % n,),
        device_id_type=MESH,
    )
    next_copy.start()
    z_total = mul(
        mul(sub_back[3], weights(sub_back[2])), weights(mul(sub_back[1], weights(sub_back[0])))
    )
    z_waiting = send(1, 0, z_bufs, z_total)

    eye = jnp.where(
        lax.broadcasted_iota(jnp.int32, (S, S), 0) == lax.broadcasted_iota(jnp.int32, (S, S), 1),
        1.0,
        0.0,
    ).astype(F32)
    identity = jnp.concatenate([eye, jnp.zeros((8, S), F32), jnp.ones((8, S), F32)], axis=0)

    prefix = None
    suffixes = [None]
    w_later = []
    for level, (radix, stride) in enumerate(levels):
        digit = digits[level]
        last = level == count - 1
        if level > 0:
            below, lower = levels[level - 1][0], digits[level - 1]
            for copy in z_waiting:
                copy.wait_recv()
            z = [z_bufs[level - 1][k] for k in range(below)]
            w_z = [weights(z[k]) for k in range(below - 1)]
            w_later.append(w_z)
            run = z[below - 1]
            options = [eye]
            for k in range(below - 2, -1, -1):
                options.insert(0, run)
                run = mul(run, w_z[k])
            z_waiting = send(1, level, z_bufs, run)
            suffix = pick(lower, options)
            if suffixes[-1] is not None:
                suffix = mul(suffix, weights(suffixes[-1]))
            suffixes.append(suffix)
        for copy in waiting:
            copy.wait_recv()
        m = [f_bufs[level][k] for k in range(radix)]
        if not last:
            if radix == 2:
                options = [identity, m[0]]
                total = compose(m[0], m[1])
            else:
                first = compose(m[0], m[1])
                total = compose(first, compose(m[2], m[3]))
                options = [identity, m[0], first, compose(first, m[2])]
            waiting = send(0, level + 1, f_bufs, total)
            here = pick(digit, options)
            prefix = here if prefix is None else compose(here, prefix)
        else:
            state = parts(m[0])[1]
            options = [jnp.zeros((8, S), F32), state]
            for k in range(1, radix - 1):
                one_map, one_add, one_decay = parts(m[k])
                state = mul(state * one_decay, weights(one_map)) + one_add
                options.append(state)
            own_map, own_add, own_decay = parts(prefix)
            entering = mul(pick(digit, options) * own_decay, weights(own_map)) + own_add

    starts = [entering]
    for b in range(SUBS - 1):
        one_map, one_add, one_decay = parts(sub[b])
        starts.append(mul(starts[-1] * one_decay, weights(one_map)) + one_add)
    x = jnp.concatenate([s[:Q] for s in starts], axis=0)
    for i in range(length):
        x = mul(x * at(dx_ref, i), w_closed) + at(u_ref, i)
        for b in range(SUBS):
            filt_ref[(b * length + i) * Q : (b * length + i + 1) * Q, :] = x[b * Q : (b + 1) * Q]

    next_copy.wait_recv()
    following = jnp.where(me == n - 1, 0.0, next_ref[:1, :])
    dx_ref[steps * Q : (steps + 1) * Q, :] = spread(following, Q)
    ahead_decay = dx_ref[Q : (steps + 1) * Q, :]
    filtered = filt_ref[...]
    predicted = mul(filtered * ahead_decay, w_trans)
    g_ref[...] = filtered - mul(predicted * ahead_decay, w_gain)

    s = at(g_ref, length - 1)
    for i in range(length - 2, -1, -1):
        s = mul(s * at(dx_ref, i + 1), w_gain) + at(g_ref, i)
    s = s * at(dx_ref, 0)
    r = [padded(s[b * Q : (b + 1) * Q]) for b in range(SUBS)]
    w_sub = [weights(sub_back[b]) for b in range(SUBS)]
    y = r[SUBS - 1]
    for b in range(SUBS - 2, -1, -1):
        y = mul(y, w_sub[b]) + r[b]

    arriving = None
    for level, (radix, stride) in enumerate(levels):
        last = level == count - 1
        y_waiting = send(2, level, y_bufs, y)
        if last:
            for copy in z_waiting:
                copy.wait_recv()
            w_later.append([weights(z_bufs[level][k]) for k in range(radix - 1)])
        for copy in y_waiting:
            copy.wait_recv()
        run = y_bufs[level][radix - 1]
        options = [jnp.zeros((8, S), F32)]
        for k in range(radix - 2, -1, -1):
            options.insert(0, run)
            if k > 0 or not last:
                run = mul(run, w_later[level][k]) + y_bufs[level][k]
        y = run
        here = pick(digits[level], options)
        if arriving is None:
            arriving = here
        else:
            arriving = arriving + mul(here, weights(suffixes[level]))

    ends = [arriving]
    for b in range(SUBS - 1, 0, -1):
        ends.insert(0, mul(ends[0], w_sub[b]) + r[b])
    x = jnp.concatenate([e[:Q] for e in ends], axis=0)
    for i in range(length - 1, -1, -1):
        s = mul(x, w_gain) + at(g_ref, i)
        for b in range(SUBS):
            smooth_ref[(b * length + i) * Q : (b * length + i + 1) * Q, :] = s[b * Q : (b + 1) * Q]
        x = s * at(dx_ref, i)

    for copy in sent:
        copy.wait_send()
    next_copy.wait_send()


def levels_of(n):
    levels, stride = [], 1
    while stride < n:
        radix = 4 if stride > 1 and n // stride % 4 == 0 else 2
        levels.append((radix, stride))
        stride *= radix
    return levels


def solution(mesh):
    n = mesh.shape["tm"]
    levels = levels_of(n)

    def local(observations, decay, transition, obs_map, noise_precision, smoother_gain):
        steps, records, channels = observations.shape
        rows = steps * records
        out = jax.ShapeDtypeStruct((rows, S), F32)
        vmem = pl.BlockSpec(memory_space=pltpu.VMEM)
        filtered, smoothed = pl.pallas_call(
            functools.partial(kernel, n, levels),
            out_shape=(out, out),
            in_specs=[vmem] * 6,
            out_specs=(vmem, vmem),
            scratch_shapes=[
                pltpu.VMEM((rows, S), F32),
                pltpu.VMEM((rows + 8, S), F32),
                pltpu.VMEM((rows, S), F32),
                pltpu.VMEM((8, S), F32),
                pltpu.SemaphoreType.DMA,
                pltpu.SemaphoreType.DMA,
            ]
            + [pltpu.VMEM((radix, S + 16, S), F32) for radix, _ in levels]
            + [pltpu.VMEM((radix, S, S), F32) for radix, _ in levels]
            + [pltpu.VMEM((radix, 8, S), F32) for radix, _ in levels]
            + [pltpu.SemaphoreType.DMA((3, len(levels), 3))] * 2,
            compiler_params=pltpu.CompilerParams(
                collective_id=0, has_side_effects=True, vmem_limit_bytes=48 * 2**20
            ),
        )(
            observations.reshape(rows, channels),
            decay,
            transition,
            obs_map,
            noise_precision.reshape(1, channels),
            smoother_gain,
        )
        return filtered.reshape(steps, records, S), smoothed.reshape(steps, records, S)

    in_specs = (P("tm", None, None), P("tm", None), P(), P(), P(), P())
    out_specs = (P("tm", None, None), P("tm", None, None))
    return jax.shard_map(local, mesh=mesh, in_specs=in_specs, out_specs=out_specs, check_vma=False)
```

```python
import functools

import jax
import jax.numpy as jnp
from jax import lax
from jax.experimental import pallas as pl
from jax.experimental.pallas import tpu as pltpu
from jax.sharding import PartitionSpec as P

MESH = pl.DeviceIdType.MESH
F32, BF16 = jnp.float32, jnp.bfloat16
S = 128
Q = 4
SUBS = 4


def halves(x):
    high = x.astype(BF16)
    low = (x - high.astype(F32)).astype(BF16)
    return jnp.concatenate([high, low], axis=1)


def weights(m):
    both = halves(m)
    return jnp.concatenate([both, both], axis=0)


def mul(x, w):
    y = jnp.dot(halves(x), w, preferred_element_type=F32)
    return y[:, :S] + y[:, S:]


def spread(row, rows):
    return jnp.broadcast_to(row, (rows, S))


def padded(x):
    return jnp.concatenate([x, jnp.zeros((8 - x.shape[0], S), F32)], axis=0)


def parts(m):
    return m[:S], m[S : S + 8], m[S + 8 :]


def compose(earlier, later):
    later_map, later_add, later_decay = parts(later)
    y = mul(earlier[: S + 8] * later_decay[:1], weights(later_map))
    return jnp.concatenate([y[:S], y[S:] + later_add, earlier[S + 8 :]], axis=0)


def pick(index, options):
    chosen = options[0]
    for k in range(1, len(options)):
        chosen = jnp.where(index == k, options[k], chosen)
    return chosen


def kernel(
    n,
    levels,
    obs_in,
    dec_in,
    trans_in,
    map_in,
    noise_in,
    gain_in,
    filt_out,
    smooth_out,
    obs_ref,
    dec_ref,
    trans_ref,
    map_ref,
    noise_ref,
    gain_ref,
    filt_ref,
    smooth_ref,
    in_sem,
    out_sem,
    u_ref,
    dx_ref,
    g_ref,
    next_ref,
    next_send,
    next_recv,
    *rest,
):
    count = len(levels)
    f_bufs, rest = rest[: count - 1], rest[count - 1 :]
    z_bufs, y_bufs, rest = rest[:count], rest[count : 2 * count], rest[2 * count :]
    own_ref, third_ref, back_ref, edge_ref, send_sem, recv_sem, edge_send, edge_recv = rest
    fetched = [
        pltpu.make_async_copy(a, b, in_sem.at[k])
        for k, (a, b) in enumerate(
            [
                (trans_in, trans_ref),
                (map_in, map_ref),
                (noise_in, noise_ref),
                (gain_in, gain_ref),
                (dec_in, dec_ref),
                (obs_in, obs_ref),
            ]
        )
    ]
    for copy in fetched:
        copy.start()
    me = lax.axis_index("tm")
    steps = dec_ref.shape[0]
    length = steps // SUBS
    digits = [(me // stride) % radix for radix, stride in levels]

    barrier = pltpu.get_barrier_semaphore()
    greeted = 0
    for (radix, stride), digit in zip(levels, digits):
        for ahead in range(1, radix):
            other = me + ((digit + ahead) % radix - digit) * stride
            pl.semaphore_signal(barrier, inc=1, device_id=(other,), device_id_type=MESH)
            greeted += 1
    pl.semaphore_signal(barrier, inc=1, device_id=((me + 1) % n,), device_id_type=MESH)
    greeted += 1

    def send(which, level, bufs, own):
        radix, stride = levels[level]
        digit = digits[level]
        bufs[level][digit] = own
        copies = []
        for ahead in range(1, radix):
            other = me + ((digit + ahead) % radix - digit) * stride
            copy = pltpu.make_async_remote_copy(
                src_ref=bufs[level].at[digit],
                dst_ref=bufs[level].at[digit],
                send_sem=send_sem.at[which, level, ahead - 1],
                recv_sem=recv_sem.at[which, level, ahead - 1],
                device_id=(other,),
                device_id_type=MESH,
            )
            copy.start()
            copies.append(copy)
        sent.extend(copies)
        return copies

    sent = []
    for copy in fetched:
        copy.wait()
    highest = lax.Precision.HIGHEST
    trans_t, gain_t = trans_ref[...].T, gain_ref[...].T
    obs_map, noise = map_ref[...], noise_ref[...]
    closed = trans_t - jnp.dot(
        trans_t,
        jnp.dot(obs_map.T * noise, obs_map, precision=highest, preferred_element_type=F32),
        precision=highest,
        preferred_element_type=F32,
    )
    w_closed, w_gain, w_trans = weights(closed), weights(gain_t), weights(trans_t)
    u_ref[...] = jnp.dot(
        obs_ref[...] * noise, obs_map, precision=highest, preferred_element_type=F32
    )
    dec = [dec_ref[t : t + 1, :] for t in range(steps)]
    for t in range(steps):
        dx_ref[t * Q : (t + 1) * Q, :] = spread(dec[t], Q)

    def at(ref, i):
        return jnp.concatenate(
            [ref[(b * length + i) * Q : (b * length + i + 1) * Q, :] for b in range(SUBS)], axis=0
        )

    def decayed(x, i):
        return [x[b * S : (b + 1) * S] * dec[b * length + i] for b in range(SUBS)]

    maps = jnp.concatenate([closed] * SUBS, axis=0)
    adds = at(u_ref, 0)
    back = jnp.concatenate([gain_t] * SUBS, axis=0)
    for i in range(1, length):
        y = mul(jnp.concatenate(decayed(maps, i) + [adds * at(dx_ref, i)], axis=0), w_closed)
        maps, adds = y[: SUBS * S], y[SUBS * S :] + at(u_ref, i)
        back = mul(jnp.concatenate(decayed(back, length - i), axis=0), w_gain)
    sub = [
        jnp.concatenate(
            [
                maps[b * S : (b + 1) * S],
                padded(adds[b * Q : (b + 1) * Q]),
                spread(dec[b * length], 8),
            ],
            axis=0,
        )
        for b in range(SUBS)
    ]
    sub_back = decayed(back, 0)
    total = compose(compose(sub[0], sub[1]), compose(sub[2], sub[3]))

    pl.semaphore_wait(barrier, greeted)
    waiting = send(0, 0, f_bufs, total)
    next_copy = pltpu.make_async_remote_copy(
        src_ref=dec_ref.at[pl.ds(0, 8)],
        dst_ref=next_ref,
        send_sem=next_send,
        recv_sem=next_recv,
        device_id=((me + n - 1) % n,),
        device_id_type=MESH,
    )
    next_copy.start()
    z_total = mul(
        mul(sub_back[3], weights(sub_back[2])), weights(mul(sub_back[1], weights(sub_back[0])))
    )
    z_waiting = send(1, 0, z_bufs, z_total)

    eye = jnp.where(
        lax.broadcasted_iota(jnp.int32, (S, S), 0) == lax.broadcasted_iota(jnp.int32, (S, S), 1),
        1.0,
        0.0,
    ).astype(F32)
    identity = jnp.concatenate([eye, jnp.zeros((8, S), F32), jnp.ones((8, S), F32)], axis=0)

    def take_back(level, waiting, suffix):
        radix = levels[level][0]
        for copy in waiting:
            copy.wait_recv()
        z = [z_bufs[level][k] for k in range(radix)]
        w_z = [weights(z[k]) for k in range(radix - 1)]
        w_later.append(w_z)
        run = z[radix - 1]
        options = [eye]
        for k in range(radix - 2, -1, -1):
            options.insert(0, run)
            run = mul(run, w_z[k])
        here = pick(digits[level], options)
        return run, here if suffix is None else mul(here, weights(suffix))

    def along(source, target, send_at, recv_at, by):
        return pltpu.make_async_remote_copy(
            src_ref=source,
            dst_ref=target,
            send_sem=edge_send.at[send_at],
            recv_sem=edge_recv.at[recv_at],
            device_id=(me + by * levels[-1][1],),
            device_id_type=MESH,
        )

    top = digits[-1]
    first_add = along(own_ref.at[pl.ds(S, 8)], edge_ref.at[0], 0, 0, 1)
    both_add = [along(edge_ref.at[2], edge_ref.at[1], k, 1, k) for k in (1, 2)]
    third = along(own_ref, third_ref, 0, 2, 1)
    back_two = [along(back_ref, z_bufs[-1].at[2], k, 4, -k) for k in (1, 2)]
    back_one = along(back_ref, z_bufs[-1].at[1], 1, 3, -1)

    w_later, suffixes = [], [None]
    prefix = None
    for level in range(count - 1):
        radix = levels[level][0]
        for copy in waiting:
            copy.wait_recv()
        m = [f_bufs[level][k] for k in range(radix)]
        if radix == 2:
            options = [identity, m[0]]
            total = compose(m[0], m[1])
        else:
            first = compose(m[0], m[1])
            total = compose(first, compose(m[2], m[3]))
        if level < count - 2:
            waiting = send(0, level + 1, f_bufs, total)
        else:
            own_ref[...] = total

            @pl.when(top == 0)
            def _():
                first_add.start()

            @pl.when(top == 2)
            def _():
                third.start()

        if level > 0:
            z_waiting = send(1, level, z_bufs, z_total)
        if radix == 4:
            options = [identity, m[0], first, compose(first, m[2])]
        here = pick(digits[level], options)
        prefix = here if prefix is None else compose(here, prefix)
        if level < count - 2:
            z_total, suffix = take_back(level, z_waiting, suffixes[-1])
            suffixes.append(suffix)

    edge_ref[3] = jnp.zeros((8, S), F32)
    own_map, own_add, own_decay = parts(total)
    w_own = weights(own_map)

    @pl.when(top == 1)
    def _():
        first_add.wait_recv()
        state = edge_ref[0]
        edge_ref[3] = state
        edge_ref[2] = mul(state * own_decay, w_own) + own_add
        for copy in both_add:
            copy.start()

    @pl.when(top == 2)
    def _():
        both_add[0].wait_recv()
        edge_ref[3] = edge_ref[1]

    @pl.when(top == 3)
    def _():
        third.wait_recv()
        one_map, one_add, one_decay = parts(third_ref[...])
        w_one = weights(one_map)
        both_add[0].wait_recv()
        edge_ref[3] = mul(edge_ref[1] * one_decay, w_one) + one_add

    own_map, own_add, own_decay = parts(prefix)
    entering = mul(edge_ref[3] * own_decay, weights(own_map)) + own_add

    starts = [entering]
    for b in range(SUBS - 1):
        one_map, one_add, one_decay = parts(sub[b])
        starts.append(mul(starts[-1] * one_decay, weights(one_map)) + one_add)
    x = jnp.concatenate([s[:Q] for s in starts], axis=0)
    for i in range(length):
        x = mul(x * at(dx_ref, i), w_closed) + at(u_ref, i)
        for b in range(SUBS):
            filt_ref[(b * length + i) * Q : (b * length + i + 1) * Q, :] = x[b * Q : (b + 1) * Q]

    filt_copy = pltpu.make_async_copy(filt_ref, filt_out, out_sem.at[0])
    filt_copy.start()
    next_copy.wait_recv()
    following = jnp.where(me == n - 1, 0.0, next_ref[:1, :])
    dx_ref[steps * Q : (steps + 1) * Q, :] = spread(following, Q)
    ahead_decay = dx_ref[Q : (steps + 1) * Q, :]
    filtered = filt_ref[...]
    predicted = mul(filtered * ahead_decay, w_trans)
    g_ref[...] = filtered - mul(predicted * ahead_decay, w_gain)

    z_total, suffix = take_back(count - 2, z_waiting, suffixes[-1])
    suffixes.append(suffix)
    back_ref[...] = z_total

    @pl.when(top == 2)
    def _():
        for copy in back_two:
            copy.start()

    @pl.when(top == 1)
    def _():
        back_one.start()

    s = at(g_ref, length - 1)
    for i in range(length - 2, -1, -1):
        s = mul(s * at(dx_ref, i + 1), w_gain) + at(g_ref, i)
    s = s * at(dx_ref, 0)
    r = [padded(s[b * Q : (b + 1) * Q]) for b in range(SUBS)]
    w_sub = [weights(sub_back[b]) for b in range(SUBS)]
    y = r[SUBS - 1]
    for b in range(SUBS - 2, -1, -1):
        y = mul(y, w_sub[b]) + r[b]

    arriving = None
    for level, (radix, stride) in enumerate(levels):
        last = level == count - 1
        y_waiting = send(2, level, y_bufs, y)
        if last:

            @pl.when(top <= 1)
            def _():
                back_two[0].wait_recv()

            @pl.when(top == 0)
            def _():
                back_one.wait_recv()

            w_later.append([None] + [weights(z_bufs[level][k]) for k in range(1, radix - 1)])
        for copy in y_waiting:
            copy.wait_recv()
        run = y_bufs[level][radix - 1]
        options = [jnp.zeros((8, S), F32)]
        for k in range(radix - 2, -1, -1):
            options.insert(0, run)
            if k > 0 or not last:
                run = mul(run, w_later[level][k]) + y_bufs[level][k]
        y = run
        here = pick(digits[level], options)
        if arriving is None:
            arriving = here
        else:
            arriving = arriving + mul(here, weights(suffixes[level]))

    ends = [arriving]
    for b in range(SUBS - 1, 0, -1):
        ends.insert(0, mul(ends[0], w_sub[b]) + r[b])
    x = jnp.concatenate([e[:Q] for e in ends], axis=0)
    for i in range(length - 1, -1, -1):
        s = mul(x, w_gain) + at(g_ref, i)
        for b in range(SUBS):
            smooth_ref[(b * length + i) * Q : (b * length + i + 1) * Q, :] = s[b * Q : (b + 1) * Q]
        x = s * at(dx_ref, i)

    smooth_copy = pltpu.make_async_copy(smooth_ref, smooth_out, out_sem.at[1])
    smooth_copy.start()
    @pl.when(top == 0)
    def _():
        first_add.wait_send()

    @pl.when(top == 1)
    def _():
        back_one.wait_send()
        for copy in both_add:
            copy.wait_send()

    @pl.when(top == 2)
    def _():
        third.wait_send()
        for copy in back_two:
            copy.wait_send()

    for copy in sent:
        copy.wait_send()
    next_copy.wait_send()
    filt_copy.wait()
    smooth_copy.wait()


def levels_of(n):
    levels, stride = [], 1
    while stride < n:
        radix = 4 if stride > 1 and n // stride % 4 == 0 else 2
        levels.append((radix, stride))
        stride *= radix
    return levels


def solution(mesh):
    n = mesh.shape["tm"]
    levels = levels_of(n)

    def local(observations, decay, transition, obs_map, noise_precision, smoother_gain):
        steps, records, channels = observations.shape
        rows = steps * records
        out = jax.ShapeDtypeStruct((rows, S), F32)
        hbm = pl.BlockSpec(memory_space=pltpu.MemorySpace.HBM)
        filtered, smoothed = pl.pallas_call(
            functools.partial(kernel, n, levels),
            out_shape=(out, out),
            in_specs=[hbm] * 6,
            out_specs=(hbm, hbm),
            scratch_shapes=[
                pltpu.VMEM((rows, channels), F32),
                pltpu.VMEM(decay.shape, F32),
                pltpu.VMEM((S, S), F32),
                pltpu.VMEM(obs_map.shape, F32),
                pltpu.VMEM((1, channels), F32),
                pltpu.VMEM((S, S), F32),
                pltpu.VMEM((rows, S), F32),
                pltpu.VMEM((rows, S), F32),
                pltpu.SemaphoreType.DMA((6,)),
                pltpu.SemaphoreType.DMA((2,)),
                pltpu.VMEM((rows, S), F32),
                pltpu.VMEM((rows + 8, S), F32),
                pltpu.VMEM((rows, S), F32),
                pltpu.VMEM((8, S), F32),
                pltpu.SemaphoreType.DMA,
                pltpu.SemaphoreType.DMA,
            ]
            + [pltpu.VMEM((radix, S + 16, S), F32) for radix, _ in levels[:-1]]
            + [pltpu.VMEM((radix, S, S), F32) for radix, _ in levels]
            + [pltpu.VMEM((radix, 8, S), F32) for radix, _ in levels]
            + [
                pltpu.VMEM((S + 16, S), F32),
                pltpu.VMEM((S + 16, S), F32),
                pltpu.VMEM((S, S), F32),
                pltpu.VMEM((4, 8, S), F32),
            ]
            + [pltpu.SemaphoreType.DMA((3, len(levels), 3))] * 2
            + [pltpu.SemaphoreType.DMA((3,)), pltpu.SemaphoreType.DMA((5,))],
            compiler_params=pltpu.CompilerParams(
                collective_id=0, has_side_effects=True, vmem_limit_bytes=63 * 2**20
            ),
        )(
            observations.reshape(rows, channels),
            decay,
            transition,
            obs_map,
            noise_precision.reshape(1, channels),
            smoother_gain,
        )
        return filtered.reshape(steps, records, S), smoothed.reshape(steps, records, S)

    in_specs = (P("tm", None, None), P("tm", None), P(), P(), P(), P())
    out_specs = (P("tm", None, None), P("tm", None, None))
    return jax.shard_map(local, mesh=mesh, in_specs=in_specs, out_specs=out_specs, check_vma=False)
```

```python
import functools

import jax
import jax.numpy as jnp
from jax import lax
from jax.experimental import pallas as pl
from jax.experimental.pallas import tpu as pltpu
from jax.sharding import PartitionSpec as P

MESH = pl.DeviceIdType.MESH
F32, BF16 = jnp.float32, jnp.bfloat16
S = 128
Q = 4
SUBS = 4


def halves(x):
    high = x.astype(BF16)
    low = (x - high.astype(F32)).astype(BF16)
    return jnp.concatenate([high, low], axis=1)


def weights(m):
    both = halves(m)
    return jnp.concatenate([both, both], axis=0)


def mul(x, w):
    y = jnp.dot(halves(x), w, preferred_element_type=F32)
    return y[:, :S] + y[:, S:]


def spread(row, rows):
    return jnp.broadcast_to(row, (rows, S))


def padded(x):
    return jnp.concatenate([x, jnp.zeros((8 - x.shape[0], S), F32)], axis=0)


def parts(m):
    return m[:S], m[S : S + 8], m[S + 8 :]


def compose(earlier, later):
    later_map, later_add, later_decay = parts(later)
    y = mul(earlier[: S + 8] * later_decay[:1], weights(later_map))
    return jnp.concatenate([y[:S], y[S:] + later_add, earlier[S + 8 :]], axis=0)


def pick(index, options):
    chosen = options[0]
    for k in range(1, len(options)):
        chosen = jnp.where(index == k, options[k], chosen)
    return chosen


def kernel(
    n,
    levels,
    obs_in,
    dec_in,
    trans_in,
    map_in,
    noise_in,
    gain_in,
    filt_out,
    smooth_out,
    obs_ref,
    dec_ref,
    trans_ref,
    map_ref,
    noise_ref,
    gain_ref,
    filt_ref,
    smooth_ref,
    in_sem,
    out_sem,
    u_ref,
    dx_ref,
    g_ref,
    next_ref,
    next_send,
    next_recv,
    *rest,
):
    count = len(levels)
    f_bufs, rest = rest[: count - 1], rest[count - 1 :]
    z_bufs, y_bufs, rest = rest[:count], rest[count : 2 * count], rest[2 * count :]
    own_ref, third_ref, edge_ref, send_sem, recv_sem, edge_send, edge_recv = rest
    fetched = [
        pltpu.make_async_copy(a, b, in_sem.at[k])
        for k, (a, b) in enumerate(
            [
                (trans_in, trans_ref),
                (map_in, map_ref),
                (noise_in, noise_ref),
                (gain_in, gain_ref),
                (dec_in, dec_ref),
                (obs_in, obs_ref),
            ]
        )
    ]
    for copy in fetched:
        copy.start()
    me = lax.axis_index("tm")
    steps = dec_ref.shape[0]
    length = steps // SUBS
    digits = [(me // stride) % radix for radix, stride in levels]

    barrier = pltpu.get_barrier_semaphore()
    greeted = 0
    for (radix, stride), digit in zip(levels, digits):
        for ahead in range(1, radix):
            other = me + ((digit + ahead) % radix - digit) * stride
            pl.semaphore_signal(barrier, inc=1, device_id=(other,), device_id_type=MESH)
            greeted += 1
    pl.semaphore_signal(barrier, inc=1, device_id=((me + 1) % n,), device_id_type=MESH)
    greeted += 1

    core = me % 2
    sibling = me + 1 - 2 * core

    def half(ref, slot):
        rows = ref.shape[1] // 2
        return ref.at[slot, pl.ds(pl.multiple_of(core * rows, 8), rows)]

    def send(which, level, bufs, own):
        radix, stride = levels[level]
        digit, buf = digits[level], bufs[level]
        buf[digit] = own
        split = level > 0 and which < 2
        source = half(buf, digit) if split else buf.at[digit]
        copies, onward = [], []
        for ahead in range(1, radix):
            other = me + ((digit + ahead) % radix - digit) * stride
            copy = pltpu.make_async_remote_copy(
                src_ref=source,
                dst_ref=source,
                send_sem=send_sem.at[which, level, ahead - 1],
                recv_sem=recv_sem.at[which, level, ahead - 1],
                device_id=(other,),
                device_id_type=MESH,
            )
            copy.start()
            copies.append(copy)
            if split:
                arrived = half(buf, (digit - ahead) % radix)
                onward.append(
                    pltpu.make_async_remote_copy(
                        src_ref=arrived,
                        dst_ref=arrived,
                        send_sem=send_sem.at[which, level, 2 + ahead],
                        recv_sem=recv_sem.at[which, level, 2 + ahead],
                        device_id=(sibling,),
                        device_id_type=MESH,
                    )
                )
        sent.extend(copies + onward)
        return copies, onward

    def relay(exchange):
        copies, onward = exchange
        for copy, more in zip(copies, onward):
            copy.wait_recv()
            more.start()

    def collect(exchange):
        copies, onward = exchange
        for copy in onward or copies:
            copy.wait_recv()

    sent = []
    for copy in fetched:
        copy.wait()
    highest = lax.Precision.HIGHEST
    trans_t, gain_t = trans_ref[...].T, gain_ref[...].T
    obs_map, noise = map_ref[...], noise_ref[...]
    closed = trans_t - jnp.dot(
        trans_t,
        jnp.dot(obs_map.T * noise, obs_map, precision=highest, preferred_element_type=F32),
        precision=highest,
        preferred_element_type=F32,
    )
    w_closed, w_gain, w_trans = weights(closed), weights(gain_t), weights(trans_t)
    u_ref[...] = jnp.dot(
        obs_ref[...] * noise, obs_map, precision=highest, preferred_element_type=F32
    )
    dec = [dec_ref[t : t + 1, :] for t in range(steps)]
    for t in range(steps):
        dx_ref[t * Q : (t + 1) * Q, :] = spread(dec[t], Q)

    def at(ref, i):
        return jnp.concatenate(
            [ref[(b * length + i) * Q : (b * length + i + 1) * Q, :] for b in range(SUBS)], axis=0
        )

    def decayed(x, i):
        return [x[b * S : (b + 1) * S] * dec[b * length + i] for b in range(SUBS)]

    maps = jnp.concatenate([closed] * SUBS, axis=0)
    adds = at(u_ref, 0)
    back = jnp.concatenate([gain_t] * SUBS, axis=0)
    for i in range(1, length):
        y = mul(jnp.concatenate(decayed(maps, i) + [adds * at(dx_ref, i)], axis=0), w_closed)
        maps, adds = y[: SUBS * S], y[SUBS * S :] + at(u_ref, i)
        back = mul(jnp.concatenate(decayed(back, length - i), axis=0), w_gain)
    sub = [
        jnp.concatenate(
            [
                maps[b * S : (b + 1) * S],
                padded(adds[b * Q : (b + 1) * Q]),
                spread(dec[b * length], 8),
            ],
            axis=0,
        )
        for b in range(SUBS)
    ]
    sub_back = decayed(back, 0)
    total = compose(compose(sub[0], sub[1]), compose(sub[2], sub[3]))

    pl.semaphore_wait(barrier, greeted)
    waiting = send(0, 0, f_bufs, total)
    next_copy = pltpu.make_async_remote_copy(
        src_ref=dec_ref.at[pl.ds(0, 8)],
        dst_ref=next_ref,
        send_sem=next_send,
        recv_sem=next_recv,
        device_id=((me + n - 1) % n,),
        device_id_type=MESH,
    )
    next_copy.start()
    z_total = mul(
        mul(sub_back[3], weights(sub_back[2])), weights(mul(sub_back[1], weights(sub_back[0])))
    )
    z_waiting = send(1, 0, z_bufs, z_total)

    eye = jnp.where(
        lax.broadcasted_iota(jnp.int32, (S, S), 0) == lax.broadcasted_iota(jnp.int32, (S, S), 1),
        1.0,
        0.0,
    ).astype(F32)
    identity = jnp.concatenate([eye, jnp.zeros((8, S), F32), jnp.ones((8, S), F32)], axis=0)

    def take_back(level, waiting, suffix):
        radix = levels[level][0]
        collect(waiting)
        z = [z_bufs[level][k] for k in range(radix)]
        w_z = [weights(z[k]) for k in range(radix - 1)]
        w_later.append(w_z)
        run = z[radix - 1]
        options = [eye]
        for k in range(radix - 2, -1, -1):
            options.insert(0, run)
            run = mul(run, w_z[k])
        here = pick(digits[level], options)
        return run, here if suffix is None else mul(here, weights(suffix))

    def along(source, target, send_at, recv_at, by):
        return pltpu.make_async_remote_copy(
            src_ref=source,
            dst_ref=target,
            send_sem=edge_send.at[send_at],
            recv_sem=edge_recv.at[recv_at],
            device_id=(me + by * levels[-1][1],),
            device_id_type=MESH,
        )

    top = digits[-1]
    first_add = along(own_ref.at[pl.ds(S, 8)], edge_ref.at[0], 0, 0, 1)
    both_add = [along(edge_ref.at[2], edge_ref.at[1], k, 1, k) for k in (1, 2)]
    third = along(own_ref, third_ref, 0, 2, 1)
    back_two = [along(half(z_bufs[-1], 2), half(z_bufs[-1], 2), k, 4, -k) for k in (1, 2)]
    back_one = along(half(z_bufs[-1], 1), half(z_bufs[-1], 1), 1, 3, -1)
    back_more = [
        pltpu.make_async_remote_copy(
            src_ref=half(z_bufs[-1], slot),
            dst_ref=half(z_bufs[-1], slot),
            send_sem=edge_send.at[2 + slot],
            recv_sem=edge_recv.at[4 + slot],
            device_id=(sibling,),
            device_id_type=MESH,
        )
        for slot in (1, 2)
    ]

    w_later, suffixes = [], [None]
    prefix = None
    for level in range(count - 1):
        radix = levels[level][0]
        relay(waiting)
        collect(waiting)
        m = [f_bufs[level][k] for k in range(radix)]
        if radix == 2:
            options = [identity, m[0]]
            total = compose(m[0], m[1])
        else:
            first = compose(m[0], m[1])
            total = compose(first, compose(m[2], m[3]))
        if level < count - 2:
            waiting = send(0, level + 1, f_bufs, total)
        else:
            own_ref[...] = total

            @pl.when(top == 0)
            def _():
                first_add.start()

            @pl.when(top == 2)
            def _():
                third.start()

        if level > 0:
            z_waiting = send(1, level, z_bufs, z_total)
        if radix == 4:
            options = [identity, m[0], first, compose(first, m[2])]
        here = pick(digits[level], options)
        prefix = here if prefix is None else compose(here, prefix)
        if level < count - 2:
            relay(z_waiting)
            z_total, suffix = take_back(level, z_waiting, suffixes[-1])
            suffixes.append(suffix)

    edge_ref[3] = jnp.zeros((8, S), F32)
    own_map, own_add, own_decay = parts(total)
    w_own = weights(own_map)

    @pl.when(top == 1)
    def _():
        first_add.wait_recv()
        state = edge_ref[0]
        edge_ref[3] = state
        edge_ref[2] = mul(state * own_decay, w_own) + own_add
        for copy in both_add:
            copy.start()

    @pl.when(top == 2)
    def _():
        both_add[0].wait_recv()
        edge_ref[3] = edge_ref[1]

    @pl.when(top == 3)
    def _():
        third.wait_recv()
        one_map, one_add, one_decay = parts(third_ref[...])
        w_one = weights(one_map)
        both_add[0].wait_recv()
        edge_ref[3] = mul(edge_ref[1] * one_decay, w_one) + one_add

    own_map, own_add, own_decay = parts(prefix)
    entering = mul(edge_ref[3] * own_decay, weights(own_map)) + own_add

    relay(z_waiting)
    starts = [entering]
    for b in range(SUBS - 1):
        one_map, one_add, one_decay = parts(sub[b])
        starts.append(mul(starts[-1] * one_decay, weights(one_map)) + one_add)
    x = jnp.concatenate([s[:Q] for s in starts], axis=0)
    for i in range(length):
        x = mul(x * at(dx_ref, i), w_closed) + at(u_ref, i)
        for b in range(SUBS):
            filt_ref[(b * length + i) * Q : (b * length + i + 1) * Q, :] = x[b * Q : (b + 1) * Q]

    filt_copy = pltpu.make_async_copy(filt_ref, filt_out, out_sem.at[0])
    filt_copy.start()
    next_copy.wait_recv()
    following = jnp.where(me == n - 1, 0.0, next_ref[:1, :])
    dx_ref[steps * Q : (steps + 1) * Q, :] = spread(following, Q)
    ahead_decay = dx_ref[Q : (steps + 1) * Q, :]
    filtered = filt_ref[...]
    predicted = mul(filtered * ahead_decay, w_trans)
    g_ref[...] = filtered - mul(predicted * ahead_decay, w_gain)

    z_total, suffix = take_back(count - 2, z_waiting, suffixes[-1])
    suffixes.append(suffix)

    @pl.when(top == 2)
    def _():
        z_bufs[-1][2] = z_total
        for copy in back_two:
            copy.start()

    @pl.when(top == 1)
    def _():
        z_bufs[-1][1] = z_total
        back_one.start()

    s = at(g_ref, length - 1)
    for i in range(length - 2, -1, -1):
        s = mul(s * at(dx_ref, i + 1), w_gain) + at(g_ref, i)
    s = s * at(dx_ref, 0)
    r = [padded(s[b * Q : (b + 1) * Q]) for b in range(SUBS)]
    w_sub = [weights(sub_back[b]) for b in range(SUBS)]
    y = r[SUBS - 1]
    for b in range(SUBS - 2, -1, -1):
        y = mul(y, w_sub[b]) + r[b]

    arriving = None
    for level, (radix, stride) in enumerate(levels):
        last = level == count - 1
        y_waiting = send(2, level, y_bufs, y)
        if level == count - 2:

            @pl.when(top <= 1)
            def _():
                back_two[0].wait_recv()
                back_more[1].start()

            @pl.when(top == 0)
            def _():
                back_one.wait_recv()
                back_more[0].start()

        if last:

            @pl.when(top <= 1)
            def _():
                back_more[1].wait_recv()

            @pl.when(top == 0)
            def _():
                back_more[0].wait_recv()

            w_later.append([None] + [weights(z_bufs[level][k]) for k in range(1, radix - 1)])
        collect(y_waiting)
        run = y_bufs[level][radix - 1]
        options = [jnp.zeros((8, S), F32)]
        for k in range(radix - 2, -1, -1):
            options.insert(0, run)
            if k > 0 or not last:
                run = mul(run, w_later[level][k]) + y_bufs[level][k]
        y = run
        here = pick(digits[level], options)
        if arriving is None:
            arriving = here
        else:
            arriving = arriving + mul(here, weights(suffixes[level]))

    ends = [arriving]
    for b in range(SUBS - 1, 0, -1):
        ends.insert(0, mul(ends[0], w_sub[b]) + r[b])
    x = jnp.concatenate([e[:Q] for e in ends], axis=0)
    for i in range(length - 1, -1, -1):
        s = mul(x, w_gain) + at(g_ref, i)
        for b in range(SUBS):
            smooth_ref[(b * length + i) * Q : (b * length + i + 1) * Q, :] = s[b * Q : (b + 1) * Q]
        x = s * at(dx_ref, i)

    smooth_copy = pltpu.make_async_copy(smooth_ref, smooth_out, out_sem.at[1])
    smooth_copy.start()
    @pl.when(top <= 1)
    def _():
        back_more[1].wait_send()

    @pl.when(top == 0)
    def _():
        first_add.wait_send()
        back_more[0].wait_send()

    @pl.when(top == 1)
    def _():
        back_one.wait_send()
        for copy in both_add:
            copy.wait_send()

    @pl.when(top == 2)
    def _():
        third.wait_send()
        for copy in back_two:
            copy.wait_send()

    for copy in sent:
        copy.wait_send()
    next_copy.wait_send()
    filt_copy.wait()
    smooth_copy.wait()


def levels_of(n):
    levels, stride = [], 1
    while stride < n:
        radix = 4 if stride > 1 and n // stride % 4 == 0 else 2
        levels.append((radix, stride))
        stride *= radix
    return levels


def solution(mesh):
    n = mesh.shape["tm"]
    levels = levels_of(n)

    def local(observations, decay, transition, obs_map, noise_precision, smoother_gain):
        steps, records, channels = observations.shape
        rows = steps * records
        out = jax.ShapeDtypeStruct((rows, S), F32)
        hbm = pl.BlockSpec(memory_space=pltpu.MemorySpace.HBM)
        filtered, smoothed = pl.pallas_call(
            functools.partial(kernel, n, levels),
            out_shape=(out, out),
            in_specs=[hbm] * 6,
            out_specs=(hbm, hbm),
            scratch_shapes=[
                pltpu.VMEM((rows, channels), F32),
                pltpu.VMEM(decay.shape, F32),
                pltpu.VMEM((S, S), F32),
                pltpu.VMEM(obs_map.shape, F32),
                pltpu.VMEM((1, channels), F32),
                pltpu.VMEM((S, S), F32),
                pltpu.VMEM((rows, S), F32),
                pltpu.VMEM((rows, S), F32),
                pltpu.SemaphoreType.DMA((6,)),
                pltpu.SemaphoreType.DMA((2,)),
                pltpu.VMEM((rows, S), F32),
                pltpu.VMEM((rows + 8, S), F32),
                pltpu.VMEM((rows, S), F32),
                pltpu.VMEM((8, S), F32),
                pltpu.SemaphoreType.DMA,
                pltpu.SemaphoreType.DMA,
            ]
            + [pltpu.VMEM((radix, S + 16, S), F32) for radix, _ in levels[:-1]]
            + [pltpu.VMEM((radix, S, S), F32) for radix, _ in levels]
            + [pltpu.VMEM((radix, 8, S), F32) for radix, _ in levels]
            + [
                pltpu.VMEM((S + 16, S), F32),
                pltpu.VMEM((S + 16, S), F32),
                pltpu.VMEM((4, 8, S), F32),
            ]
            + [pltpu.SemaphoreType.DMA((3, len(levels), 6))] * 2
            + [pltpu.SemaphoreType.DMA((5,)), pltpu.SemaphoreType.DMA((7,))],
            compiler_params=pltpu.CompilerParams(
                collective_id=0, has_side_effects=True, vmem_limit_bytes=63 * 2**20
            ),
        )(
            observations.reshape(rows, channels),
            decay,
            transition,
            obs_map,
            noise_precision.reshape(1, channels),
            smoother_gain,
        )
        return filtered.reshape(steps, records, S), smoothed.reshape(steps, records, S)

    in_specs = (P("tm", None, None), P("tm", None), P(), P(), P(), P())
    out_specs = (P("tm", None, None), P("tm", None, None))
    return jax.shard_map(local, mesh=mesh, in_specs=in_specs, out_specs=out_specs, check_vma=False)
```

```python
import functools

import jax
import jax.numpy as jnp
from jax import lax
from jax.experimental import pallas as pl
from jax.experimental.pallas import tpu as pltpu
from jax.sharding import PartitionSpec as P

MESH = pl.DeviceIdType.MESH
F32, BF16 = jnp.float32, jnp.bfloat16
S = 128
Q = 4
SUBS = 4


def halves(x):
    high = x.astype(BF16)
    low = (x - high.astype(F32)).astype(BF16)
    return jnp.concatenate([high, low], axis=1)


def weights(m):
    both = halves(m)
    return jnp.concatenate([both, both], axis=0)


def mul(x, w):
    y = jnp.dot(halves(x), w, preferred_element_type=F32)
    return y[:, :S] + y[:, S:]


def spread(row, rows):
    return jnp.broadcast_to(row, (rows, S))


def padded(x):
    return jnp.concatenate([x, jnp.zeros((8 - x.shape[0], S), F32)], axis=0)


def parts(m):
    return m[:S], m[S : S + 8], m[S + 8 :]


def compose(earlier, later):
    later_map, later_add, later_decay = parts(later)
    y = mul(earlier[: S + 8] * later_decay[:1], weights(later_map))
    return jnp.concatenate([y[:S], y[S:] + later_add, earlier[S + 8 :]], axis=0)


def pick(index, options):
    chosen = options[0]
    for k in range(1, len(options)):
        chosen = jnp.where(index == k, options[k], chosen)
    return chosen


def kernel(
    n,
    levels,
    obs_in,
    dec_in,
    trans_in,
    map_in,
    noise_in,
    gain_in,
    filt_out,
    smooth_out,
    obs_ref,
    dec_ref,
    trans_ref,
    map_ref,
    noise_ref,
    gain_ref,
    filt_ref,
    smooth_ref,
    in_sem,
    out_sem,
    u_ref,
    dx_ref,
    g_ref,
    next_ref,
    next_send,
    next_recv,
    *rest,
):
    count = len(levels)
    f_bufs, rest = rest[: count - 1], rest[count - 1 :]
    z_bufs, y_bufs, rest = rest[:count], rest[count : 2 * count], rest[2 * count :]
    own_ref, third_ref, edge_ref, send_sem, recv_sem, edge_send, edge_recv = rest
    fetched = [
        pltpu.make_async_copy(a, b, in_sem.at[k])
        for k, (a, b) in enumerate(
            [
                (trans_in, trans_ref),
                (map_in, map_ref),
                (noise_in, noise_ref),
                (gain_in, gain_ref),
                (dec_in, dec_ref),
                (obs_in, obs_ref),
            ]
        )
    ]
    for copy in fetched:
        copy.start()
    me = lax.axis_index("tm")
    steps = dec_ref.shape[0]
    length = steps // SUBS
    digits = [(me // stride) % radix for radix, stride in levels]

    barrier = pltpu.get_barrier_semaphore()
    greeted = 0
    for (radix, stride), digit in zip(levels, digits):
        for ahead in range(1, radix):
            other = me + ((digit + ahead) % radix - digit) * stride
            pl.semaphore_signal(barrier, inc=1, device_id=(other,), device_id_type=MESH)
            greeted += 1
    pl.semaphore_signal(barrier, inc=1, device_id=((me + 1) % n,), device_id_type=MESH)
    greeted += 1

    core = me % 2
    sibling = me + 1 - 2 * core

    def half(ref, slot):
        rows = ref.shape[1] // 2
        return ref.at[slot, pl.ds(pl.multiple_of(core * rows, 8), rows)]

    def send(which, level, bufs, own):
        radix, stride = levels[level]
        digit, buf = digits[level], bufs[level]
        buf[digit] = own
        split = level > 0 and which < 2
        source = half(buf, digit) if split else buf.at[digit]
        copies, onward = [], []
        for ahead in range(1, radix):
            other = me + ((digit + ahead) % radix - digit) * stride
            copy = pltpu.make_async_remote_copy(
                src_ref=source,
                dst_ref=source,
                send_sem=send_sem.at[which, level, ahead - 1],
                recv_sem=recv_sem.at[which, level, ahead - 1],
                device_id=(other,),
                device_id_type=MESH,
            )
            copy.start()
            copies.append(copy)
            if split:
                arrived = half(buf, (digit - ahead) % radix)
                onward.append(
                    pltpu.make_async_remote_copy(
                        src_ref=arrived,
                        dst_ref=arrived,
                        send_sem=send_sem.at[which, level, 2 + ahead],
                        recv_sem=recv_sem.at[which, level, 2 + ahead],
                        device_id=(sibling,),
                        device_id_type=MESH,
                    )
                )
        sent.extend(copies + onward)
        return copies, onward

    def relay(exchange):
        copies, onward = exchange
        for copy, more in zip(copies, onward):
            copy.wait_recv()
            more.start()

    def collect(exchange):
        copies, onward = exchange
        for copy in onward or copies:
            copy.wait_recv()

    sent = []
    for copy in fetched:
        copy.wait()
    highest = lax.Precision.HIGHEST
    trans_t, gain_t = trans_ref[...].T, gain_ref[...].T
    obs_map, noise = map_ref[...], noise_ref[...]
    closed = trans_t - jnp.dot(
        trans_t,
        jnp.dot(obs_map.T * noise, obs_map, precision=highest, preferred_element_type=F32),
        precision=highest,
        preferred_element_type=F32,
    )
    w_closed, w_gain, w_trans = weights(closed), weights(gain_t), weights(trans_t)
    u_ref[...] = jnp.dot(
        obs_ref[...] * noise, obs_map, precision=highest, preferred_element_type=F32
    )
    dec = [dec_ref[t : t + 1, :] for t in range(steps)]
    for t in range(steps):
        dx_ref[t * Q : (t + 1) * Q, :] = spread(dec[t], Q)

    def at(ref, i):
        return jnp.concatenate(
            [ref[(b * length + i) * Q : (b * length + i + 1) * Q, :] for b in range(SUBS)], axis=0
        )

    def decayed(x, i):
        return [x[b * S : (b + 1) * S] * dec[b * length + i] for b in range(SUBS)]

    maps = jnp.concatenate([closed] * SUBS, axis=0)
    adds = at(u_ref, 0)
    back = jnp.concatenate([gain_t] * SUBS, axis=0)
    for i in range(1, length):
        y = mul(jnp.concatenate(decayed(maps, i) + [adds * at(dx_ref, i)], axis=0), w_closed)
        maps, adds = y[: SUBS * S], y[SUBS * S :] + at(u_ref, i)
        back = mul(jnp.concatenate(decayed(back, length - i), axis=0), w_gain)
    sub = [
        jnp.concatenate(
            [
                maps[b * S : (b + 1) * S],
                padded(adds[b * Q : (b + 1) * Q]),
                spread(dec[b * length], 8),
            ],
            axis=0,
        )
        for b in range(SUBS)
    ]
    sub_back = decayed(back, 0)
    total = compose(compose(sub[0], sub[1]), compose(sub[2], sub[3]))

    pl.semaphore_wait(barrier, greeted)
    waiting = send(0, 0, f_bufs, total)
    next_copy = pltpu.make_async_remote_copy(
        src_ref=dec_ref.at[pl.ds(0, 8)],
        dst_ref=next_ref,
        send_sem=next_send,
        recv_sem=next_recv,
        device_id=((me + n - 1) % n,),
        device_id_type=MESH,
    )
    next_copy.start()
    z_total = mul(
        mul(sub_back[3], weights(sub_back[2])), weights(mul(sub_back[1], weights(sub_back[0])))
    )
    z_waiting = send(1, 0, z_bufs, z_total)

    eye = jnp.where(
        lax.broadcasted_iota(jnp.int32, (S, S), 0) == lax.broadcasted_iota(jnp.int32, (S, S), 1),
        1.0,
        0.0,
    ).astype(F32)
    identity = jnp.concatenate([eye, jnp.zeros((8, S), F32), jnp.ones((8, S), F32)], axis=0)

    def take_back(level, waiting, suffix):
        radix = levels[level][0]
        collect(waiting)
        z = [z_bufs[level][k] for k in range(radix)]
        w_z = [weights(z[k]) for k in range(radix - 1)]
        w_later.append(w_z)
        run = z[radix - 1]
        options = [eye]
        for k in range(radix - 2, -1, -1):
            options.insert(0, run)
            run = mul(run, w_z[k])
        here = pick(digits[level], options)
        return run, here if suffix is None else mul(here, weights(suffix))

    def along(source, target, send_at, recv_at, by):
        return pltpu.make_async_remote_copy(
            src_ref=source,
            dst_ref=target,
            send_sem=edge_send.at[send_at],
            recv_sem=edge_recv.at[recv_at],
            device_id=(me + by * levels[-1][1],),
            device_id_type=MESH,
        )

    top = digits[-1]
    first_add = along(own_ref.at[pl.ds(S, 8)], edge_ref.at[0], 0, 0, 1)
    both_add = [along(edge_ref.at[2], edge_ref.at[1], k, 1, k) for k in (1, 2)]
    third = along(own_ref, third_ref, 0, 2, 1)
    back_two = [along(half(z_bufs[-1], 2), half(z_bufs[-1], 2), k, 4, -k) for k in (1, 2)]
    back_one = along(half(z_bufs[-1], 1), half(z_bufs[-1], 1), 1, 3, -1)
    back_more = [
        pltpu.make_async_remote_copy(
            src_ref=half(z_bufs[-1], slot),
            dst_ref=half(z_bufs[-1], slot),
            send_sem=edge_send.at[2 + slot],
            recv_sem=edge_recv.at[4 + slot],
            device_id=(sibling,),
            device_id_type=MESH,
        )
        for slot in (1, 2)
    ]

    w_later, suffixes = [], [None]
    prefix = None
    for level in range(count - 1):
        radix = levels[level][0]
        if level > 0:
            z_waiting = send(1, level, z_bufs, z_total)
        relay(waiting)
        collect(waiting)
        m = [f_bufs[level][k] for k in range(radix)]
        if radix == 2:
            options = [identity, m[0]]
            total = compose(m[0], m[1])
        else:
            first = compose(m[0], m[1])
            total = compose(first, compose(m[2], m[3]))
        if level < count - 2:
            waiting = send(0, level + 1, f_bufs, total)
        else:
            own_ref[...] = total

            @pl.when(top == 0)
            def _():
                first_add.start()

            @pl.when(top == 2)
            def _():
                third.start()

        if radix == 4:
            options = [identity, m[0], first, compose(first, m[2])]
        here = pick(digits[level], options)
        prefix = here if prefix is None else compose(here, prefix)
        if level < count - 2:
            relay(z_waiting)
            z_total, suffix = take_back(level, z_waiting, suffixes[-1])
            suffixes.append(suffix)

    edge_ref[3] = jnp.zeros((8, S), F32)
    own_map, own_add, own_decay = parts(total)
    w_own = weights(own_map)

    @pl.when(top == 1)
    def _():
        first_add.wait_recv()
        state = edge_ref[0]
        edge_ref[3] = state
        edge_ref[2] = mul(state * own_decay, w_own) + own_add
        for copy in both_add:
            copy.start()

    @pl.when(top == 2)
    def _():
        both_add[0].wait_recv()
        edge_ref[3] = edge_ref[1]

    @pl.when(top == 3)
    def _():
        third.wait_recv()
        one_map, one_add, one_decay = parts(third_ref[...])
        w_one = weights(one_map)
        both_add[0].wait_recv()
        edge_ref[3] = mul(edge_ref[1] * one_decay, w_one) + one_add

    own_map, own_add, own_decay = parts(prefix)
    entering = mul(edge_ref[3] * own_decay, weights(own_map)) + own_add

    relay(z_waiting)
    starts = [entering]
    for b in range(SUBS - 1):
        one_map, one_add, one_decay = parts(sub[b])
        starts.append(mul(starts[-1] * one_decay, weights(one_map)) + one_add)
    x = jnp.concatenate([s[:Q] for s in starts], axis=0)
    for i in range(length):
        x = mul(x * at(dx_ref, i), w_closed) + at(u_ref, i)
        for b in range(SUBS):
            filt_ref[(b * length + i) * Q : (b * length + i + 1) * Q, :] = x[b * Q : (b + 1) * Q]

    filt_copy = pltpu.make_async_copy(filt_ref, filt_out, out_sem.at[0])
    filt_copy.start()
    next_copy.wait_recv()
    following = jnp.where(me == n - 1, 0.0, next_ref[:1, :])
    dx_ref[steps * Q : (steps + 1) * Q, :] = spread(following, Q)
    ahead_decay = dx_ref[Q : (steps + 1) * Q, :]
    filtered = filt_ref[...]
    predicted = mul(filtered * ahead_decay, w_trans)
    g_ref[...] = filtered - mul(predicted * ahead_decay, w_gain)

    z_total, suffix = take_back(count - 2, z_waiting, suffixes[-1])
    suffixes.append(suffix)

    @pl.when(top == 2)
    def _():
        z_bufs[-1][2] = z_total
        for copy in back_two:
            copy.start()

    @pl.when(top == 1)
    def _():
        z_bufs[-1][1] = z_total
        back_one.start()

    s = at(g_ref, length - 1)
    for i in range(length - 2, -1, -1):
        s = mul(s * at(dx_ref, i + 1), w_gain) + at(g_ref, i)
    s = s * at(dx_ref, 0)
    r = [padded(s[b * Q : (b + 1) * Q]) for b in range(SUBS)]
    w_sub = [weights(sub_back[b]) for b in range(SUBS)]
    y = r[SUBS - 1]
    for b in range(SUBS - 2, -1, -1):
        y = mul(y, w_sub[b]) + r[b]

    arriving = None
    for level, (radix, stride) in enumerate(levels):
        last = level == count - 1
        y_waiting = send(2, level, y_bufs, y)
        if level == count - 2:

            @pl.when(top <= 1)
            def _():
                back_two[0].wait_recv()
                back_more[1].start()

            @pl.when(top == 0)
            def _():
                back_one.wait_recv()
                back_more[0].start()

        if last:

            @pl.when(top <= 1)
            def _():
                back_more[1].wait_recv()

            @pl.when(top == 0)
            def _():
                back_more[0].wait_recv()

            w_later.append([None] + [weights(z_bufs[level][k]) for k in range(1, radix - 1)])
        collect(y_waiting)
        run = y_bufs[level][radix - 1]
        options = [jnp.zeros((8, S), F32)]
        for k in range(radix - 2, -1, -1):
            options.insert(0, run)
            if k > 0 or not last:
                run = mul(run, w_later[level][k]) + y_bufs[level][k]
        y = run
        here = pick(digits[level], options)
        if arriving is None:
            arriving = here
        else:
            arriving = arriving + mul(here, weights(suffixes[level]))

    ends = [arriving]
    for b in range(SUBS - 1, 0, -1):
        ends.insert(0, mul(ends[0], w_sub[b]) + r[b])
    x = jnp.concatenate([e[:Q] for e in ends], axis=0)
    for i in range(length - 1, -1, -1):
        s = mul(x, w_gain) + at(g_ref, i)
        for b in range(SUBS):
            smooth_ref[(b * length + i) * Q : (b * length + i + 1) * Q, :] = s[b * Q : (b + 1) * Q]
        x = s * at(dx_ref, i)

    smooth_copy = pltpu.make_async_copy(smooth_ref, smooth_out, out_sem.at[1])
    smooth_copy.start()
    @pl.when(top <= 1)
    def _():
        back_more[1].wait_send()

    @pl.when(top == 0)
    def _():
        first_add.wait_send()
        back_more[0].wait_send()

    @pl.when(top == 1)
    def _():
        back_one.wait_send()
        for copy in both_add:
            copy.wait_send()

    @pl.when(top == 2)
    def _():
        third.wait_send()
        for copy in back_two:
            copy.wait_send()

    for copy in sent:
        copy.wait_send()
    next_copy.wait_send()
    filt_copy.wait()
    smooth_copy.wait()


def levels_of(n):
    levels, stride = [], 1
    while stride < n:
        radix = 4 if stride > 1 and n // stride % 4 == 0 else 2
        levels.append((radix, stride))
        stride *= radix
    return levels


def solution(mesh):
    n = mesh.shape["tm"]
    levels = levels_of(n)

    def local(observations, decay, transition, obs_map, noise_precision, smoother_gain):
        steps, records, channels = observations.shape
        rows = steps * records
        out = jax.ShapeDtypeStruct((rows, S), F32)
        hbm = pl.BlockSpec(memory_space=pltpu.MemorySpace.HBM)
        filtered, smoothed = pl.pallas_call(
            functools.partial(kernel, n, levels),
            out_shape=(out, out),
            in_specs=[hbm] * 6,
            out_specs=(hbm, hbm),
            scratch_shapes=[
                pltpu.VMEM((rows, channels), F32),
                pltpu.VMEM(decay.shape, F32),
                pltpu.VMEM((S, S), F32),
                pltpu.VMEM(obs_map.shape, F32),
                pltpu.VMEM((1, channels), F32),
                pltpu.VMEM((S, S), F32),
                pltpu.VMEM((rows, S), F32),
                pltpu.VMEM((rows, S), F32),
                pltpu.SemaphoreType.DMA((6,)),
                pltpu.SemaphoreType.DMA((2,)),
                pltpu.VMEM((rows, S), F32),
                pltpu.VMEM((rows + 8, S), F32),
                pltpu.VMEM((rows, S), F32),
                pltpu.VMEM((8, S), F32),
                pltpu.SemaphoreType.DMA,
                pltpu.SemaphoreType.DMA,
            ]
            + [pltpu.VMEM((radix, S + 16, S), F32) for radix, _ in levels[:-1]]
            + [pltpu.VMEM((radix, S, S), F32) for radix, _ in levels]
            + [pltpu.VMEM((radix, 8, S), F32) for radix, _ in levels]
            + [
                pltpu.VMEM((S + 16, S), F32),
                pltpu.VMEM((S + 16, S), F32),
                pltpu.VMEM((4, 8, S), F32),
            ]
            + [pltpu.SemaphoreType.DMA((3, len(levels), 6))] * 2
            + [pltpu.SemaphoreType.DMA((5,)), pltpu.SemaphoreType.DMA((7,))],
            compiler_params=pltpu.CompilerParams(
                collective_id=0, has_side_effects=True, vmem_limit_bytes=63 * 2**20
            ),
        )(
            observations.reshape(rows, channels),
            decay,
            transition,
            obs_map,
            noise_precision.reshape(1, channels),
            smoother_gain,
        )
        return filtered.reshape(steps, records, S), smoothed.reshape(steps, records, S)

    in_specs = (P("tm", None, None), P("tm", None), P(), P(), P(), P())
    out_specs = (P("tm", None, None), P("tm", None, None))
    return jax.shard_map(local, mesh=mesh, in_specs=in_specs, out_specs=out_specs, check_vma=False)
```

```python
import functools

import jax
import jax.numpy as jnp
from jax import lax
from jax.experimental import pallas as pl
from jax.experimental.pallas import tpu as pltpu
from jax.sharding import PartitionSpec as P

MESH = pl.DeviceIdType.MESH
F32, BF16 = jnp.float32, jnp.bfloat16
S = 128
Q = 4
SUBS = 4


def halves(x):
    high = x.astype(BF16)
    low = (x - high.astype(F32)).astype(BF16)
    return jnp.concatenate([high, low], axis=1)


def weights(m):
    both = halves(m)
    return jnp.concatenate([both, both], axis=0)


def mul(x, w):
    y = jnp.dot(halves(x), w, preferred_element_type=F32)
    return y[:, :S] + y[:, S:]


def spread(row, rows):
    return jnp.broadcast_to(row, (rows, S))


def padded(x):
    return jnp.concatenate([x, jnp.zeros((8 - x.shape[0], S), F32)], axis=0)


def parts(m):
    return m[:S], m[S : S + 8], m[S + 8 :]


def compose(earlier, later):
    later_map, later_add, later_decay = parts(later)
    y = mul(earlier[: S + 8] * later_decay[:1], weights(later_map))
    return jnp.concatenate([y[:S], y[S:] + later_add, earlier[S + 8 :]], axis=0)


def pick(index, options):
    chosen = options[0]
    for k in range(1, len(options)):
        chosen = jnp.where(index == k, options[k], chosen)
    return chosen


def kernel(
    n,
    levels,
    obs_in,
    dec_in,
    trans_in,
    map_in,
    noise_in,
    gain_in,
    filt_out,
    smooth_out,
    obs_ref,
    dec_ref,
    trans_ref,
    map_ref,
    noise_ref,
    gain_ref,
    filt_ref,
    smooth_ref,
    in_sem,
    out_sem,
    u_ref,
    dx_ref,
    g_ref,
    next_ref,
    next_send,
    next_recv,
    *rest,
):
    count = len(levels)
    f_bufs, rest = rest[: count - 1], rest[count - 1 :]
    z_bufs, y_bufs, rest = rest[:count], rest[count : 2 * count], rest[2 * count :]
    own_ref, third_ref, back_ref, edge_ref, send_sem, recv_sem, edge_send, edge_recv = rest
    fetched = [
        pltpu.make_async_copy(a, b, in_sem.at[k])
        for k, (a, b) in enumerate(
            [
                (trans_in, trans_ref),
                (map_in, map_ref),
                (noise_in, noise_ref),
                (gain_in, gain_ref),
                (dec_in, dec_ref),
                (obs_in, obs_ref),
            ]
        )
    ]
    for copy in fetched:
        copy.start()
    me = lax.axis_index("tm")
    steps = dec_ref.shape[0]
    length = steps // SUBS
    digits = [(me // stride) % radix for radix, stride in levels]

    barrier = pltpu.get_barrier_semaphore()
    greeted = 0
    for (radix, stride), digit in zip(levels, digits):
        for ahead in range(1, radix):
            other = me + ((digit + ahead) % radix - digit) * stride
            pl.semaphore_signal(barrier, inc=1, device_id=(other,), device_id_type=MESH)
            greeted += 1
    pl.semaphore_signal(barrier, inc=1, device_id=((me + 1) % n,), device_id_type=MESH)
    greeted += 1

    def send(which, level, bufs, own):
        radix, stride = levels[level]
        digit = digits[level]
        bufs[level][digit] = own
        copies = []
        for ahead in range(1, radix):
            other = me + ((digit + ahead) % radix - digit) * stride
            copy = pltpu.make_async_remote_copy(
                src_ref=bufs[level].at[digit],
                dst_ref=bufs[level].at[digit],
                send_sem=send_sem.at[which, level, ahead - 1],
                recv_sem=recv_sem.at[which, level, ahead - 1],
                device_id=(other,),
                device_id_type=MESH,
            )
            copy.start()
            copies.append(copy)
        sent.extend(copies)
        return copies

    sent = []
    for copy in fetched:
        copy.wait()
    highest = lax.Precision.HIGHEST
    trans_t, gain_t = trans_ref[...].T, gain_ref[...].T
    obs_map, noise = map_ref[...], noise_ref[...]
    closed = trans_t - jnp.dot(
        trans_t,
        jnp.dot(obs_map.T * noise, obs_map, precision=highest, preferred_element_type=F32),
        precision=highest,
        preferred_element_type=F32,
    )
    w_closed, w_gain, w_trans = weights(closed), weights(gain_t), weights(trans_t)
    u_ref[...] = jnp.dot(
        obs_ref[...] * noise, obs_map, precision=highest, preferred_element_type=F32
    )
    dec = [dec_ref[t : t + 1, :] for t in range(steps)]
    for t in range(steps):
        dx_ref[t * Q : (t + 1) * Q, :] = spread(dec[t], Q)

    def at(ref, i):
        return jnp.concatenate(
            [ref[(b * length + i) * Q : (b * length + i + 1) * Q, :] for b in range(SUBS)], axis=0
        )

    def decayed(x, i):
        return [x[b * S : (b + 1) * S] * dec[b * length + i] for b in range(SUBS)]

    maps = jnp.concatenate([closed] * SUBS, axis=0)
    adds = at(u_ref, 0)
    back = jnp.concatenate([gain_t] * SUBS, axis=0)
    for i in range(1, length):
        y = mul(jnp.concatenate(decayed(maps, i) + [adds * at(dx_ref, i)], axis=0), w_closed)
        maps, adds = y[: SUBS * S], y[SUBS * S :] + at(u_ref, i)
        back = mul(jnp.concatenate(decayed(back, length - i), axis=0), w_gain)
    sub = [
        jnp.concatenate(
            [
                maps[b * S : (b + 1) * S],
                padded(adds[b * Q : (b + 1) * Q]),
                spread(dec[b * length], 8),
            ],
            axis=0,
        )
        for b in range(SUBS)
    ]
    sub_back = decayed(back, 0)
    total = compose(compose(sub[0], sub[1]), compose(sub[2], sub[3]))

    pl.semaphore_wait(barrier, greeted)
    waiting = send(0, 0, f_bufs, total)
    next_copy = pltpu.make_async_remote_copy(
        src_ref=dec_ref.at[pl.ds(0, 8)],
        dst_ref=next_ref,
        send_sem=next_send,
        recv_sem=next_recv,
        device_id=((me + n - 1) % n,),
        device_id_type=MESH,
    )
    next_copy.start()
    z_total = mul(
        mul(sub_back[3], weights(sub_back[2])), weights(mul(sub_back[1], weights(sub_back[0])))
    )
    z_waiting = send(1, 0, z_bufs, z_total)

    eye = jnp.where(
        lax.broadcasted_iota(jnp.int32, (S, S), 0) == lax.broadcasted_iota(jnp.int32, (S, S), 1),
        1.0,
        0.0,
    ).astype(F32)
    identity = jnp.concatenate([eye, jnp.zeros((8, S), F32), jnp.ones((8, S), F32)], axis=0)

    def take_back(level, waiting, suffix):
        radix = levels[level][0]
        for copy in waiting:
            copy.wait_recv()
        z = [z_bufs[level][k] for k in range(radix)]
        w_z = [weights(z[k]) for k in range(radix - 1)]
        w_later.append(w_z)
        run = z[radix - 1]
        options = [eye]
        for k in range(radix - 2, -1, -1):
            options.insert(0, run)
            run = mul(run, w_z[k])
        here = pick(digits[level], options)
        return run, here if suffix is None else mul(here, weights(suffix))

    def along(source, target, send_at, recv_at, by):
        return pltpu.make_async_remote_copy(
            src_ref=source,
            dst_ref=target,
            send_sem=edge_send.at[send_at],
            recv_sem=edge_recv.at[recv_at],
            device_id=(me + by * levels[-1][1],),
            device_id_type=MESH,
        )

    top = digits[-1]
    first_add = along(own_ref.at[pl.ds(S, 8)], edge_ref.at[0], 0, 0, 1)
    both_add = [along(edge_ref.at[2], edge_ref.at[1], k, 1, k) for k in (1, 2)]
    third = along(own_ref, third_ref, 0, 2, 1)
    back_two = [along(back_ref, z_bufs[-1].at[2], k, 4, -k) for k in (1, 2)]
    back_one = along(back_ref, z_bufs[-1].at[1], 1, 3, -1)

    w_later, suffixes = [], [None]
    prefix = None
    for level in range(count - 1):
        radix = levels[level][0]
        for copy in waiting:
            copy.wait_recv()
        m = [f_bufs[level][k] for k in range(radix)]
        if radix == 2:
            options = [identity, m[0]]
            total = compose(m[0], m[1])
        else:
            first = compose(m[0], m[1])
            total = compose(first, compose(m[2], m[3]))
        if level < count - 2:
            waiting = send(0, level + 1, f_bufs, total)
        else:
            own_ref[...] = total

            @pl.when(top == 0)
            def _():
                first_add.start()

            @pl.when(top == 2)
            def _():
                third.start()

        if level > 0:
            z_waiting = send(1, level, z_bufs, z_total)
        if radix == 4:
            options = [identity, m[0], first, compose(first, m[2])]
        here = pick(digits[level], options)
        prefix = here if prefix is None else compose(here, prefix)
        if level < count - 2:
            z_total, suffix = take_back(level, z_waiting, suffixes[-1])
            suffixes.append(suffix)

    edge_ref[3] = jnp.zeros((8, S), F32)
    own_map, own_add, own_decay = parts(total)
    w_own = weights(own_map)

    @pl.when(top == 1)
    def _():
        first_add.wait_recv()
        state = edge_ref[0]
        edge_ref[3] = state
        edge_ref[2] = mul(state * own_decay, w_own) + own_add
        for copy in both_add:
            copy.start()

    @pl.when(top == 2)
    def _():
        both_add[0].wait_recv()
        edge_ref[3] = edge_ref[1]

    @pl.when(top == 3)
    def _():
        third.wait_recv()
        one_map, one_add, one_decay = parts(third_ref[...])
        w_one = weights(one_map)
        both_add[0].wait_recv()
        edge_ref[3] = mul(edge_ref[1] * one_decay, w_one) + one_add

    own_map, own_add, own_decay = parts(prefix)
    entering = mul(edge_ref[3] * own_decay, weights(own_map)) + own_add

    starts = [entering]
    for b in range(SUBS - 1):
        one_map, one_add, one_decay = parts(sub[b])
        starts.append(mul(starts[-1] * one_decay, weights(one_map)) + one_add)
    x = jnp.concatenate([s[:Q] for s in starts], axis=0)
    for i in range(length):
        x = mul(x * at(dx_ref, i), w_closed) + at(u_ref, i)
        for b in range(SUBS):
            filt_ref[(b * length + i) * Q : (b * length + i + 1) * Q, :] = x[b * Q : (b + 1) * Q]

    filt_copy = pltpu.make_async_copy(filt_ref, filt_out, out_sem.at[0])
    filt_copy.start()
    next_copy.wait_recv()
    following = jnp.where(me == n - 1, 0.0, next_ref[:1, :])
    dx_ref[steps * Q : (steps + 1) * Q, :] = spread(following, Q)
    ahead_decay = dx_ref[Q : (steps + 1) * Q, :]
    filtered = filt_ref[...]
    predicted = mul(filtered * ahead_decay, w_trans)
    g_ref[...] = filtered - mul(predicted * ahead_decay, w_gain)

    z_total, suffix = take_back(count - 2, z_waiting, suffixes[-1])
    suffixes.append(suffix)
    back_ref[...] = z_total

    @pl.when(top == 2)
    def _():
        for copy in back_two:
            copy.start()

    @pl.when(top == 1)
    def _():
        back_one.start()

    s = at(g_ref, length - 1)
    for i in range(length - 2, -1, -1):
        s = mul(s * at(dx_ref, i + 1), w_gain) + at(g_ref, i)
    s = s * at(dx_ref, 0)
    r = [padded(s[b * Q : (b + 1) * Q]) for b in range(SUBS)]
    w_sub = [weights(sub_back[b]) for b in range(SUBS)]
    y = r[SUBS - 1]
    for b in range(SUBS - 2, -1, -1):
        y = mul(y, w_sub[b]) + r[b]

    arriving = None
    for level, (radix, stride) in enumerate(levels):
        last = level == count - 1
        y_waiting = send(2, level, y_bufs, y)
        if last:

            @pl.when(top <= 1)
            def _():
                back_two[0].wait_recv()

            @pl.when(top == 0)
            def _():
                back_one.wait_recv()

            w_later.append([None] + [weights(z_bufs[level][k]) for k in range(1, radix - 1)])
        for copy in y_waiting:
            copy.wait_recv()
        run = y_bufs[level][radix - 1]
        options = [jnp.zeros((8, S), F32)]
        for k in range(radix - 2, -1, -1):
            options.insert(0, run)
            if k > 0 or not last:
                run = mul(run, w_later[level][k]) + y_bufs[level][k]
        y = run
        here = pick(digits[level], options)
        if arriving is None:
            arriving = here
        else:
            arriving = arriving + mul(here, weights(suffixes[level]))

    ends = [arriving]
    for b in range(SUBS - 1, 0, -1):
        ends.insert(0, mul(ends[0], w_sub[b]) + r[b])
    x = jnp.concatenate([e[:Q] for e in ends], axis=0)
    for i in range(length - 1, -1, -1):
        s = mul(x, w_gain) + at(g_ref, i)
        for b in range(SUBS):
            smooth_ref[(b * length + i) * Q : (b * length + i + 1) * Q, :] = s[b * Q : (b + 1) * Q]
        x = s * at(dx_ref, i)

    smooth_copy = pltpu.make_async_copy(smooth_ref, smooth_out, out_sem.at[1])
    smooth_copy.start()
    @pl.when(top == 0)
    def _():
        first_add.wait_send()

    @pl.when(top == 1)
    def _():
        back_one.wait_send()
        for copy in both_add:
            copy.wait_send()

    @pl.when(top == 2)
    def _():
        third.wait_send()
        for copy in back_two:
            copy.wait_send()

    for copy in sent:
        copy.wait_send()
    next_copy.wait_send()
    filt_copy.wait()
    smooth_copy.wait()


def place(filt_in, smooth_in, filt_out, smooth_out, sem):
    copies = [
        pltpu.make_async_copy(filt_in, filt_out, sem.at[0]),
        pltpu.make_async_copy(smooth_in, smooth_out, sem.at[1]),
    ]
    for copy in copies:
        copy.start()
    for copy in copies:
        copy.wait()


def levels_of(n):
    levels, stride = [], 1
    while stride < n:
        radix = 4 if stride > 1 and n // stride % 4 == 0 else 2
        levels.append((radix, stride))
        stride *= radix
    return levels


def solution(mesh):
    n = mesh.shape["tm"]
    levels = levels_of(n)

    def local(observations, decay, transition, obs_map, noise_precision, smoother_gain):
        steps, records, channels = observations.shape
        rows = steps * records
        out = jax.ShapeDtypeStruct((rows, S), F32)
        hbm = pl.BlockSpec(memory_space=pltpu.MemorySpace.HBM)
        filtered, smoothed = pl.pallas_call(
            functools.partial(kernel, n, levels),
            out_shape=(out, out),
            in_specs=[hbm] * 6,
            out_specs=(hbm, hbm),
            scratch_shapes=[
                pltpu.VMEM((rows, channels), F32),
                pltpu.VMEM(decay.shape, F32),
                pltpu.VMEM((S, S), F32),
                pltpu.VMEM(obs_map.shape, F32),
                pltpu.VMEM((1, channels), F32),
                pltpu.VMEM((S, S), F32),
                pltpu.VMEM((rows, S), F32),
                pltpu.VMEM((rows, S), F32),
                pltpu.SemaphoreType.DMA((6,)),
                pltpu.SemaphoreType.DMA((2,)),
                pltpu.VMEM((rows, S), F32),
                pltpu.VMEM((rows + 8, S), F32),
                pltpu.VMEM((rows, S), F32),
                pltpu.VMEM((8, S), F32),
                pltpu.SemaphoreType.DMA,
                pltpu.SemaphoreType.DMA,
            ]
            + [pltpu.VMEM((radix, S + 16, S), F32) for radix, _ in levels[:-1]]
            + [pltpu.VMEM((radix, S, S), F32) for radix, _ in levels]
            + [pltpu.VMEM((radix, 8, S), F32) for radix, _ in levels]
            + [
                pltpu.VMEM((S + 16, S), F32),
                pltpu.VMEM((S + 16, S), F32),
                pltpu.VMEM((S, S), F32),
                pltpu.VMEM((4, 8, S), F32),
            ]
            + [pltpu.SemaphoreType.DMA((3, len(levels), 3))] * 2
            + [pltpu.SemaphoreType.DMA((3,)), pltpu.SemaphoreType.DMA((5,))],
            compiler_params=pltpu.CompilerParams(
                collective_id=0, has_side_effects=True, vmem_limit_bytes=63 * 2**20
            ),
        )(
            observations.reshape(rows, channels),
            decay,
            transition,
            obs_map,
            noise_precision.reshape(1, channels),
            smoother_gain,
        )
        filtered, smoothed = pl.pallas_call(
            place,
            out_shape=(out, out),
            in_specs=[hbm] * 2,
            out_specs=(hbm, hbm),
            scratch_shapes=[pltpu.SemaphoreType.DMA((2,))],
            compiler_params=pltpu.CompilerParams(vmem_limit_bytes=63 * 2**20),
        )(filtered, smoothed)
        return filtered.reshape(steps, records, S), smoothed.reshape(steps, records, S)

    in_specs = (P("tm", None, None), P("tm", None), P(), P(), P(), P())
    out_specs = (P("tm", None, None), P("tm", None, None))
    return jax.shard_map(local, mesh=mesh, in_specs=in_specs, out_specs=out_specs, check_vma=False)
```

```python
import functools

import jax
import jax.numpy as jnp
from jax import lax
from jax.experimental import pallas as pl
from jax.experimental.pallas import tpu as pltpu
from jax.sharding import PartitionSpec as P

MESH = pl.DeviceIdType.MESH
F32, BF16 = jnp.float32, jnp.bfloat16
S = 128
Q = 4
SUBS = 4


def halves(x):
    high = x.astype(BF16)
    low = (x - high.astype(F32)).astype(BF16)
    return jnp.concatenate([high, low], axis=1)


def weights(m):
    both = halves(m)
    return jnp.concatenate([both, both], axis=0)


def mul(x, w):
    y = jnp.dot(halves(x), w, preferred_element_type=F32)
    return y[:, :S] + y[:, S:]


def spread(row, rows):
    return jnp.broadcast_to(row, (rows, S))


def padded(x):
    return jnp.concatenate([x, jnp.zeros((8 - x.shape[0], S), F32)], axis=0)


def parts(m):
    return m[:S], m[S : S + 8], m[S + 8 :]


def compose(earlier, later):
    later_map, later_add, later_decay = parts(later)
    y = mul(earlier[: S + 8] * later_decay[:1], weights(later_map))
    return jnp.concatenate([y[:S], y[S:] + later_add, earlier[S + 8 :]], axis=0)


def pick(index, options):
    chosen = options[0]
    for k in range(1, len(options)):
        chosen = jnp.where(index == k, options[k], chosen)
    return chosen


def kernel(
    n,
    levels,
    obs_in,
    dec_in,
    trans_in,
    map_in,
    noise_in,
    gain_in,
    filt_out,
    smooth_out,
    obs_ref,
    dec_ref,
    trans_ref,
    map_ref,
    noise_ref,
    gain_ref,
    filt_ref,
    smooth_ref,
    in_sem,
    out_sem,
    u_ref,
    dx_ref,
    g_ref,
    next_ref,
    next_send,
    next_recv,
    *rest,
):
    count = len(levels)
    f_bufs, rest = rest[: count - 1], rest[count - 1 :]
    z_bufs, y_bufs, rest = rest[:count], rest[count : 2 * count], rest[2 * count :]
    own_ref, third_ref, back_ref, edge_ref, send_sem, recv_sem, edge_send, edge_recv = rest
    fetched = [
        pltpu.make_async_copy(a, b, in_sem.at[k])
        for k, (a, b) in enumerate(
            [
                (trans_in, trans_ref),
                (map_in, map_ref),
                (noise_in, noise_ref),
                (gain_in, gain_ref),
                (dec_in, dec_ref),
                (obs_in, obs_ref),
            ]
        )
    ]
    for copy in fetched:
        copy.start()
    me = lax.axis_index("tm")
    steps = dec_ref.shape[0]
    length = steps // SUBS
    digits = [(me // stride) % radix for radix, stride in levels]

    barrier = pltpu.get_barrier_semaphore()
    greeted = 0
    for (radix, stride), digit in zip(levels, digits):
        for ahead in range(1, radix):
            other = me + ((digit + ahead) % radix - digit) * stride
            pl.semaphore_signal(barrier, inc=1, device_id=(other,), device_id_type=MESH)
            greeted += 1
    pl.semaphore_signal(barrier, inc=1, device_id=((me + 1) % n,), device_id_type=MESH)
    greeted += 1

    def send(which, level, bufs, own):
        radix, stride = levels[level]
        digit = digits[level]
        bufs[level][digit] = own
        copies = []
        for ahead in range(1, radix):
            other = me + ((digit + ahead) % radix - digit) * stride
            copy = pltpu.make_async_remote_copy(
                src_ref=bufs[level].at[digit],
                dst_ref=bufs[level].at[digit],
                send_sem=send_sem.at[which, level, ahead - 1],
                recv_sem=recv_sem.at[which, level, ahead - 1],
                device_id=(other,),
                device_id_type=MESH,
            )
            copy.start()
            copies.append(copy)
        sent.extend(copies)
        return copies

    sent = []
    for copy in fetched:
        copy.wait()
    highest = lax.Precision.HIGHEST
    trans_t, gain_t = trans_ref[...].T, gain_ref[...].T
    obs_map, noise = map_ref[...], noise_ref[...]
    closed = trans_t - jnp.dot(
        trans_t,
        jnp.dot(obs_map.T * noise, obs_map, precision=highest, preferred_element_type=F32),
        precision=highest,
        preferred_element_type=F32,
    )
    w_closed, w_gain, w_trans = weights(closed), weights(gain_t), weights(trans_t)
    u_ref[...] = jnp.dot(
        obs_ref[...] * noise, obs_map, precision=highest, preferred_element_type=F32
    )
    dec = [dec_ref[t : t + 1, :] for t in range(steps)]
    for t in range(steps):
        dx_ref[t * Q : (t + 1) * Q, :] = spread(dec[t], Q)

    def at(ref, i):
        return jnp.concatenate(
            [ref[(b * length + i) * Q : (b * length + i + 1) * Q, :] for b in range(SUBS)], axis=0
        )

    def decayed(x, i):
        return [x[b * S : (b + 1) * S] * dec[b * length + i] for b in range(SUBS)]

    maps = jnp.concatenate([closed] * SUBS, axis=0)
    adds = at(u_ref, 0)
    back = jnp.concatenate([gain_t] * SUBS, axis=0)
    for i in range(1, length):
        y = mul(jnp.concatenate(decayed(maps, i) + [adds * at(dx_ref, i)], axis=0), w_closed)
        maps, adds = y[: SUBS * S], y[SUBS * S :] + at(u_ref, i)
        back = mul(jnp.concatenate(decayed(back, length - i), axis=0), w_gain)
    sub = [
        jnp.concatenate(
            [
                maps[b * S : (b + 1) * S],
                padded(adds[b * Q : (b + 1) * Q]),
                spread(dec[b * length], 8),
            ],
            axis=0,
        )
        for b in range(SUBS)
    ]
    sub_back = decayed(back, 0)
    total = compose(compose(sub[0], sub[1]), compose(sub[2], sub[3]))

    pl.semaphore_wait(barrier, greeted)
    waiting = send(0, 0, f_bufs, total)
    next_copy = pltpu.make_async_remote_copy(
        src_ref=dec_ref.at[pl.ds(0, 8)],
        dst_ref=next_ref,
        send_sem=next_send,
        recv_sem=next_recv,
        device_id=((me + n - 1) % n,),
        device_id_type=MESH,
    )
    next_copy.start()
    z_total = mul(
        mul(sub_back[3], weights(sub_back[2])), weights(mul(sub_back[1], weights(sub_back[0])))
    )
    z_waiting = send(1, 0, z_bufs, z_total)

    eye = jnp.where(
        lax.broadcasted_iota(jnp.int32, (S, S), 0) == lax.broadcasted_iota(jnp.int32, (S, S), 1),
        1.0,
        0.0,
    ).astype(F32)
    identity = jnp.concatenate([eye, jnp.zeros((8, S), F32), jnp.ones((8, S), F32)], axis=0)

    def take_back(level, waiting, suffix):
        radix = levels[level][0]
        for copy in waiting:
            copy.wait_recv()
        z = [z_bufs[level][k] for k in range(radix)]
        w_z = [weights(z[k]) for k in range(radix - 1)]
        w_later.append(w_z)
        run = z[radix - 1]
        options = [eye]
        for k in range(radix - 2, -1, -1):
            options.insert(0, run)
            run = mul(run, w_z[k])
        here = pick(digits[level], options)
        return run, here if suffix is None else mul(here, weights(suffix))

    def along(source, target, send_at, recv_at, by):
        return pltpu.make_async_remote_copy(
            src_ref=source,
            dst_ref=target,
            send_sem=edge_send.at[send_at],
            recv_sem=edge_recv.at[recv_at],
            device_id=(me + by * levels[-1][1],),
            device_id_type=MESH,
        )

    top = digits[-1]
    first_add = along(own_ref.at[pl.ds(S, 8)], edge_ref.at[0], 0, 0, 1)
    both_add = [along(edge_ref.at[2], edge_ref.at[1], k, 1, k) for k in (1, 2)]
    third = along(own_ref, third_ref, 0, 2, 1)
    back_two = [along(back_ref, z_bufs[-1].at[2], k, 4, -k) for k in (1, 2)]
    back_one = along(back_ref, z_bufs[-1].at[1], 1, 3, -1)

    w_later, suffixes = [], [None]
    prefix = None
    for level in range(count - 1):
        radix = levels[level][0]
        for copy in waiting:
            copy.wait_recv()
        m = [f_bufs[level][k] for k in range(radix)]
        if radix == 2:
            options = [identity, m[0]]
            total = compose(m[0], m[1])
        else:
            first = compose(m[0], m[1])
            total = compose(first, compose(m[2], m[3]))
        if level < count - 2:
            waiting = send(0, level + 1, f_bufs, total)
        else:
            own_ref[...] = total

            @pl.when(top == 0)
            def _():
                first_add.start()

            @pl.when(top == 2)
            def _():
                third.start()

        if level > 0:
            z_waiting = send(1, level, z_bufs, z_total)
        if radix == 4:
            options = [identity, m[0], first, compose(first, m[2])]
        here = pick(digits[level], options)
        prefix = here if prefix is None else compose(here, prefix)
        if level < count - 2:
            z_total, suffix = take_back(level, z_waiting, suffixes[-1])
            suffixes.append(suffix)

    edge_ref[3] = jnp.zeros((8, S), F32)
    own_map, own_add, own_decay = parts(total)
    w_own = weights(own_map)

    @pl.when(top == 1)
    def _():
        first_add.wait_recv()
        state = edge_ref[0]
        edge_ref[3] = state
        edge_ref[2] = mul(state * own_decay, w_own) + own_add
        for copy in both_add:
            copy.start()

    @pl.when(top == 2)
    def _():
        both_add[0].wait_recv()
        edge_ref[3] = edge_ref[1]

    @pl.when(top == 3)
    def _():
        third.wait_recv()
        one_map, one_add, one_decay = parts(third_ref[...])
        w_one = weights(one_map)
        both_add[0].wait_recv()
        edge_ref[3] = mul(edge_ref[1] * one_decay, w_one) + one_add

    own_map, own_add, own_decay = parts(prefix)
    entering = mul(edge_ref[3] * own_decay, weights(own_map)) + own_add

    starts = [entering]
    for b in range(SUBS - 1):
        one_map, one_add, one_decay = parts(sub[b])
        starts.append(mul(starts[-1] * one_decay, weights(one_map)) + one_add)
    x = jnp.concatenate([s[:Q] for s in starts], axis=0)
    for i in range(length):
        x = mul(x * at(dx_ref, i), w_closed) + at(u_ref, i)
        for b in range(SUBS):
            filt_ref[(b * length + i) * Q : (b * length + i + 1) * Q, :] = x[b * Q : (b + 1) * Q]

    filt_copy = pltpu.make_async_copy(filt_ref, filt_out, out_sem.at[0])
    filt_copy.start()
    next_copy.wait_recv()
    following = jnp.where(me == n - 1, 0.0, next_ref[:1, :])
    dx_ref[steps * Q : (steps + 1) * Q, :] = spread(following, Q)
    ahead_decay = dx_ref[Q : (steps + 1) * Q, :]
    filtered = filt_ref[...]
    predicted = mul(filtered * ahead_decay, w_trans)
    g_ref[...] = filtered - mul(predicted * ahead_decay, w_gain)

    s = at(g_ref, length - 1)
    for i in range(length - 2, -1, -1):
        s = mul(s * at(dx_ref, i + 1), w_gain) + at(g_ref, i)
    s = s * at(dx_ref, 0)
    r = [padded(s[b * Q : (b + 1) * Q]) for b in range(SUBS)]
    w_sub = [weights(sub_back[b]) for b in range(SUBS)]
    y = r[SUBS - 1]
    for b in range(SUBS - 2, -1, -1):
        y = mul(y, w_sub[b]) + r[b]

    z_total, suffix = take_back(count - 2, z_waiting, suffixes[-1])
    suffixes.append(suffix)
    back_ref[...] = z_total

    @pl.when(top == 2)
    def _():
        for copy in back_two:
            copy.start()

    @pl.when(top == 1)
    def _():
        back_one.start()

    arriving = None
    for level, (radix, stride) in enumerate(levels):
        last = level == count - 1
        y_waiting = send(2, level, y_bufs, y)
        if last:

            @pl.when(top <= 1)
            def _():
                back_two[0].wait_recv()

            @pl.when(top == 0)
            def _():
                back_one.wait_recv()

            w_later.append([None] + [weights(z_bufs[level][k]) for k in range(1, radix - 1)])
        for copy in y_waiting:
            copy.wait_recv()
        run = y_bufs[level][radix - 1]
        options = [jnp.zeros((8, S), F32)]
        for k in range(radix - 2, -1, -1):
            options.insert(0, run)
            if k > 0 or not last:
                run = mul(run, w_later[level][k]) + y_bufs[level][k]
        y = run
        here = pick(digits[level], options)
        if arriving is None:
            arriving = here
        else:
            arriving = arriving + mul(here, weights(suffixes[level]))

    ends = [arriving]
    for b in range(SUBS - 1, 0, -1):
        ends.insert(0, mul(ends[0], w_sub[b]) + r[b])
    x = jnp.concatenate([e[:Q] for e in ends], axis=0)
    for i in range(length - 1, -1, -1):
        s = mul(x, w_gain) + at(g_ref, i)
        for b in range(SUBS):
            smooth_ref[(b * length + i) * Q : (b * length + i + 1) * Q, :] = s[b * Q : (b + 1) * Q]
        x = s * at(dx_ref, i)

    smooth_copy = pltpu.make_async_copy(smooth_ref, smooth_out, out_sem.at[1])
    smooth_copy.start()
    @pl.when(top == 0)
    def _():
        first_add.wait_send()

    @pl.when(top == 1)
    def _():
        back_one.wait_send()
        for copy in both_add:
            copy.wait_send()

    @pl.when(top == 2)
    def _():
        third.wait_send()
        for copy in back_two:
            copy.wait_send()

    for copy in sent:
        copy.wait_send()
    next_copy.wait_send()
    filt_copy.wait()
    smooth_copy.wait()


def levels_of(n):
    levels, stride = [], 1
    while stride < n:
        radix = 4 if stride > 1 and n // stride % 4 == 0 else 2
        levels.append((radix, stride))
        stride *= radix
    return levels


def solution(mesh):
    n = mesh.shape["tm"]
    levels = levels_of(n)

    def local(observations, decay, transition, obs_map, noise_precision, smoother_gain):
        steps, records, channels = observations.shape
        rows = steps * records
        out = jax.ShapeDtypeStruct((rows, S), F32)
        hbm = pl.BlockSpec(memory_space=pltpu.MemorySpace.HBM)
        filtered, smoothed = pl.pallas_call(
            functools.partial(kernel, n, levels),
            out_shape=(out, out),
            in_specs=[hbm] * 6,
            out_specs=(hbm, hbm),
            scratch_shapes=[
                pltpu.VMEM((rows, channels), F32),
                pltpu.VMEM(decay.shape, F32),
                pltpu.VMEM((S, S), F32),
                pltpu.VMEM(obs_map.shape, F32),
                pltpu.VMEM((1, channels), F32),
                pltpu.VMEM((S, S), F32),
                pltpu.VMEM((rows, S), F32),
                pltpu.VMEM((rows, S), F32),
                pltpu.SemaphoreType.DMA((6,)),
                pltpu.SemaphoreType.DMA((2,)),
                pltpu.VMEM((rows, S), F32),
                pltpu.VMEM((rows + 8, S), F32),
                pltpu.VMEM((rows, S), F32),
                pltpu.VMEM((8, S), F32),
                pltpu.SemaphoreType.DMA,
                pltpu.SemaphoreType.DMA,
            ]
            + [pltpu.VMEM((radix, S + 16, S), F32) for radix, _ in levels[:-1]]
            + [pltpu.VMEM((radix, S, S), F32) for radix, _ in levels]
            + [pltpu.VMEM((radix, 8, S), F32) for radix, _ in levels]
            + [
                pltpu.VMEM((S + 16, S), F32),
                pltpu.VMEM((S + 16, S), F32),
                pltpu.VMEM((S, S), F32),
                pltpu.VMEM((4, 8, S), F32),
            ]
            + [pltpu.SemaphoreType.DMA((3, len(levels), 3))] * 2
            + [pltpu.SemaphoreType.DMA((3,)), pltpu.SemaphoreType.DMA((5,))],
            compiler_params=pltpu.CompilerParams(
                collective_id=0, has_side_effects=True, vmem_limit_bytes=63 * 2**20
            ),
        )(
            observations.reshape(rows, channels),
            decay,
            transition,
            obs_map,
            noise_precision.reshape(1, channels),
            smoother_gain,
        )
        return filtered.reshape(steps, records, S), smoothed.reshape(steps, records, S)

    in_specs = (P("tm", None, None), P("tm", None), P(), P(), P(), P())
    out_specs = (P("tm", None, None), P("tm", None, None))
    return jax.shard_map(local, mesh=mesh, in_specs=in_specs, out_specs=out_specs, check_vma=False)
```
